32 devices in a mesh: seq: 8 (over z, x), rep: 4 (over y, core).
Axes of the slice: x: 2, y: 2, z: 4, core: 2. Of those that a mesh axis runs over, the one named last changes fastest.
Arguments:
- query_in: bfloat16 [4, 1024, 1024], P('rep', 'seq'), may hold values from -120 to 120
- key_in: bfloat16 [4, 1024, 1024], P('rep', 'seq'), may hold values from -4 to 4
- value_in: bfloat16 [4, 1024, 1024], P('rep', 'seq'), may hold values from -6 to 6
- out_weight: bfloat16 [1024, 2048], replicated, may hold values from -0.1875 to 0.1875
- grad_out: bfloat16 [4, 1024, 2048], P('rep', 'seq'), may hold values from -6 to 6
- pattern: int32 [16, 8], replicated, may hold values from 0 to 15, as said below
Outputs:
- mixed_out: bfloat16 [4, 1024, 2048], P('rep', 'seq')
- query_grad: bfloat16 [4, 1024, 1024], P('rep', 'seq')
- key_grad: bfloat16 [4, 1024, 1024], P('rep', 'seq')
- value_grad: bfloat16 [4, 1024, 1024], P('rep', 'seq')
- weight_grad: float32 [1024, 2048], P('seq')
The draws below stay inside these ranges and needn't reach their ends.
Inputs may be any that keep to these rules, and one draw needn't show every extreme that they name: `pattern`: row b names blocks b - 1, b and b + 1 modulo 16 in columns 0 to 2; columns 3 and 4 hold the same two blocks in every row; the other columns may name any block.
All inputs are finite; a program needn't handle non-finite values.
Results may differ from the reference program's by a relative error of at most 0.0095.
Values may be sent and summed in bfloat16 or wider, within the bound.
No kernel may reach another device: no remote copies, remote signals or barrier semaphores. Data moves between devices by JAX's collectives and lax.ppermute only.
A program may use at most 128 MiB of HBM per device.

```python
import math
import jax
import jax.numpy as jnp
from jax import lax

HD = 128
HEADS = 8
D = 2048
BLK = 64
R = 8
DOCS = 4
TOKENS = 1024
NB = 16
GROUPS = 1


def draw_key_in(key, part):
    result = jnp.clip(jax.random.normal(jax.random.fold_in(key, 21), (DOCS, TOKENS, HEADS * HD), jnp.float32), -4.0, 4.0)
    return result.astype(jnp.bfloat16)


def draw_query_in(key, part):
    result = jnp.clip(jax.random.normal(jax.random.fold_in(key, 22), (DOCS, TOKENS, HEADS * HD), jnp.float32), -4.0, 4.0)
    return result.astype(jnp.bfloat16)


def draw_pattern(key, part):
    blocks = jnp.arange(NB, dtype=jnp.int32)
    window = jnp.stack([(blocks + NB - 1) % NB, blocks, (blocks + 1) % NB], axis=1)
    global_ids = jax.random.randint(jax.random.fold_in(key, 31), (1, 2), 0, NB, dtype=jnp.int32)
    global_cols = jnp.broadcast_to(global_ids, (NB, 2))
    random_cols = jax.random.randint(jax.random.fold_in(key, 32), (NB, R - 5), 0, NB, dtype=jnp.int32)
    return jnp.concatenate([window, global_cols, random_cols], axis=1).astype(jnp.int32)


def steps_of(stream_key, shape, split, least, top_value):
    gain, own = 1.0, jax.random.fold_in(stream_key, 6)
    for position, blocks in split:
        draws = jnp.exp(jax.random.uniform(jax.random.fold_in(own, position), (blocks,), jnp.float32, least / len(split), top_value / len(split)))
        gain = gain * jnp.repeat(draws, shape[position] // blocks).reshape([-1 if axis == position else 1 for axis in range(len(shape))])
    return gain


def bell_draw(rng, extent, scale, bound, split=(), kind=jnp.bfloat16):
    values = jax.random.normal(rng, extent, jnp.float32) * scale
    if len(split) > 0:
        values = steps_of(rng, extent, split, -0.22, 0.18) * values
    return jnp.clip(values, min=-bound, max=bound).astype(kind)


def setup_inputs(seed: int = 0) -> dict:
    key_of = jax.random.split(jax.random.key(seed), 7)
    return {
        "query_in": draw_query_in(jax.random.fold_in(key_of[6], 71), 0),
        "key_in": draw_key_in(jax.random.fold_in(key_of[6], 71), 0),
        "value_in": bell_draw(key_of[2], (DOCS, TOKENS, HEADS * HD), 1.0, 6.0, ((0, 4), (1, 8))),
        "out_weight": bell_draw(key_of[3], (HEADS * HD, D), (HEADS * HD) ** -0.5, 0.1875),
        "grad_out": bell_draw(key_of[4], (DOCS, TOKENS, D), 1.0, 6.0, ((0, 4), (1, 8))),
        "pattern": draw_pattern(jax.random.fold_in(key_of[6], 71), 0),
    }


def gather_blocks(blocks, pattern):
    return blocks[pattern].reshape(NB, R * BLK, HD)

def softmax_rows(queries, gathered):
    scores = jnp.einsum('nqd,nkd->nqk', queries.astype(jnp.float32), gathered.astype(jnp.float32)) * (1.0 / math.sqrt(HD))
    shifted = scores - lax.optimization_barrier(jnp.max(scores, axis=-1, keepdims=True))
    weights = jnp.exp(shifted)
    return weights / lax.optimization_barrier(jnp.sum(weights, axis=-1, keepdims=True))

def head_forward(queries, keys_head, values_head, pattern):
    key_gathered = gather_blocks(keys_head, pattern)
    value_gathered = gather_blocks(values_head, pattern)
    probs = softmax_rows(queries, key_gathered)
    probs_low = probs.astype(jnp.bfloat16)
    result = jnp.einsum('nqk,nkd->nqd', probs_low.astype(jnp.float32), value_gathered.astype(jnp.float32))
    return result.astype(jnp.bfloat16)

def round_sum(parts):
    rounded = lax.optimization_barrier(parts.astype(jnp.bfloat16))
    return lax.optimization_barrier(jnp.sum(rounded.astype(jnp.float32), axis=0)).astype(jnp.bfloat16)

def scatter_parts(contrib, pattern):
    shaped = contrib.reshape(GROUPS, NB, R, BLK, HD)
    return jnp.zeros((GROUPS, NB, BLK, HD), jnp.float32).at[:, pattern].add(shaped)

def head_backward(queries, keys_head, values_head, out_grad, pattern):
    scale = 1.0 / math.sqrt(HD)
    key_gathered = gather_blocks(keys_head, pattern)
    value_gathered = gather_blocks(values_head, pattern)
    probs = softmax_rows(queries, key_gathered)
    probs_low = probs.astype(jnp.bfloat16)
    prob_grad = jnp.einsum('nqd,nkd->nqk', out_grad.astype(jnp.float32), value_gathered.astype(jnp.float32))
    delta = lax.optimization_barrier(jnp.sum(probs * prob_grad, axis=-1, keepdims=True))
    score_grad = (probs * (prob_grad - delta)).astype(jnp.bfloat16)
    query_part = jnp.einsum('nqk,nkd->nqd', score_grad.astype(jnp.float32), key_gathered.astype(jnp.float32)) * scale
    group_rows = BLK // GROUPS
    score_groups = score_grad.reshape(NB, GROUPS, group_rows, R * BLK).astype(jnp.float32)
    query_groups = queries.reshape(NB, GROUPS, group_rows, HD).astype(jnp.float32)
    prob_groups = probs_low.reshape(NB, GROUPS, group_rows, R * BLK).astype(jnp.float32)
    grad_groups = out_grad.reshape(NB, GROUPS, group_rows, HD).astype(jnp.float32)
    key_contrib = jnp.einsum('ngqk,ngqd->gnkd', score_groups, query_groups) * scale
    value_contrib = jnp.einsum('ngqk,ngqd->gnkd', prob_groups, grad_groups)
    key_total = round_sum(scatter_parts(key_contrib, pattern))
    value_total = round_sum(scatter_parts(value_contrib, pattern))
    return (query_part.astype(jnp.bfloat16), key_total, value_total)

def split_heads(source):
    return source.reshape(DOCS, NB, BLK, HEADS, HD).transpose(0, 3, 1, 2, 4).reshape(DOCS * HEADS, NB, BLK, HD)

def merge_heads(source):
    return source.reshape(DOCS, HEADS, NB, BLK, HD).transpose(0, 2, 3, 1, 4).reshape(DOCS, TOKENS, HEADS * HD)

def reference(query_in, key_in, value_in, out_weight, grad_out, pattern):
    query_split = split_heads(query_in)
    key_split = split_heads(key_in)
    value_split = split_heads(value_in)
    attended = merge_heads(lax.map(lambda items: head_forward(items[0], items[1], items[2], pattern), (query_split, key_split, value_split)))
    flat_attended = attended.reshape(DOCS * TOKENS, HEADS * HD)
    flat_grad = grad_out.reshape(DOCS * TOKENS, D)
    mixed_out = jnp.dot(flat_attended, out_weight, preferred_element_type=jnp.float32).astype(jnp.bfloat16).reshape(DOCS, TOKENS, D)
    attended_grad = jnp.dot(flat_grad, out_weight.T, preferred_element_type=jnp.float32).astype(jnp.bfloat16)
    weight_grad = jnp.dot(flat_attended.T, flat_grad, preferred_element_type=jnp.float32) * (1.0 / math.sqrt(DOCS * TOKENS))
    grad_split = split_heads(attended_grad.reshape(DOCS, TOKENS, HEADS * HD))
    query_heads, key_heads, value_heads = lax.map(lambda items: head_backward(items[0], items[1], items[2], items[3], pattern), (query_split, key_split, value_split, grad_split))
    return (mixed_out, merge_heads(query_heads), merge_heads(key_heads), merge_heads(value_heads), weight_grad)
```

```python
import functools
import math

import jax
import jax.numpy as jnp
from jax import lax
from jax.experimental import pallas as pl
from jax.experimental.pallas import tpu as pltpu
from jax.sharding import PartitionSpec as P

HD = 128
BLK = 64
MASKED = -1e30
VMEM = pltpu.VMEM
NT = (((1,), (1,)), ((), ()))
NN = (((1,), (0,)), ((), ()))
TN = (((0,), (0,)), ((), ()))


def dot(left, right, dims):
    return lax.dot_general(left, right, dims, preferred_element_type=jnp.float32)


def whole(count):
    return [pl.BlockSpec(memory_space=VMEM)] * count


def params(mib):
    return pltpu.CompilerParams(vmem_limit_bytes=mib * 1024 * 1024)


def cost(flops, moved):
    return pl.CostEstimate(flops=flops, bytes_accessed=moved, transcendentals=0)


def struct(*shape, dtype=jnp.bfloat16):
    return jax.ShapeDtypeStruct(shape, dtype)


def swap(array, axis, mask):
    return lax.ppermute(array, axis, [(i, i ^ mask) for i in range(lax.axis_size(axis))])


def pack_kernel(ids, key_ref, value_ref, query_ref, *sends):
    for mask, send in enumerate(sends):
        columns = pl.ds(pl.multiple_of((ids[0] ^ mask) * HD, HD), HD)
        rows = key_ref.shape[0]
        send[:rows] = key_ref[:, columns]
        send[rows : 2 * rows] = value_ref[:, columns]
        send[2 * rows :] = query_ref[:, columns]


def pack(ids, key_local, value_local, query_local, peers):
    rows = key_local.shape[0]
    return pl.pallas_call(
        pack_kernel,
        out_shape=[struct(3 * rows, HD)] * peers,
        in_specs=[pl.BlockSpec(memory_space=pltpu.SMEM)] + whole(3),
        out_specs=whole(peers),
        compiler_params=params(16),
        name="pack_kvq",
    )(ids, key_local, value_local, query_local)


def quarter_kernel(ids, grad_ref, *sends):
    width = grad_ref.shape[1] // len(sends)
    for mask, send in enumerate(sends):
        send[...] = grad_ref[:, pl.ds(pl.multiple_of((ids[1] ^ mask) * width, width), width)]


def quarters(ids, grad_local, count):
    rows, width = grad_local.shape
    return pl.pallas_call(
        quarter_kernel,
        out_shape=[struct(rows, width // count)] * count,
        in_specs=[pl.BlockSpec(memory_space=pltpu.SMEM)] + whole(1),
        out_specs=whole(count),
        compiler_params=params(16),
        name="pack_grad",
    )(ids, grad_local)


def head_grad_kernel(ids, grad_ref, weight_ref, *sends):
    step = pl.program_id(0)
    block = dot(grad_ref[...], weight_ref[...], NT).astype(jnp.bfloat16)
    for mask, send in enumerate(sends):

        @pl.when(step == mask)
        def _():
            send[...] = block


def head_grads(ids, grad_local, out_weight, peers):
    rows, width = grad_local.shape
    grid = pltpu.PrefetchScalarGridSpec(
        num_scalar_prefetch=1,
        grid=(peers,),
        in_specs=[
            pl.BlockSpec((rows, width), lambda i, ids: (0, 0)),
            pl.BlockSpec((HD, width), lambda i, ids: (ids[0] ^ i, 0)),
        ],
        out_specs=[pl.BlockSpec((rows, HD), lambda i, ids: (0, 0))] * peers,
    )
    return pl.pallas_call(
        head_grad_kernel,
        out_shape=[struct(rows, HD)] * peers,
        grid_spec=grid,
        compiler_params=params(16),
        cost_estimate=cost(2 * rows * width * HD * peers, out_weight.size * 2),
        name="head_grads",
    )(ids, grad_local, out_weight)


def load_heads(ids, parts, rows, *targets):
    for mask, part in enumerate(parts):
        place = pl.ds(pl.multiple_of((ids[0] ^ mask) * rows, rows), rows)
        for index, target in enumerate(targets):
            target[place] = part[index * rows : (index + 1) * rows]


def scores_of(keys, queries, bias, scale):
    blocks = bias.shape[0]
    scores = dot(keys, queries, NT) * scale
    shaped = scores.reshape(blocks, BLK, queries.shape[0]) + bias[:, None, :]
    return shaped.reshape(scores.shape)


def forward_kernel(peers, chunk, scale, ids, bias_ref, *refs):
    parts, refs = refs[:peers], refs[peers:]
    outs, (top_ref, sum_ref, keys, values, queries, heads) = refs[:-6], refs[-6:]
    load_heads(ids, parts, parts[0].shape[0] // 3, keys, values, queries)
    value_cols = values[...].T
    for start in range(0, keys.shape[0], chunk):
        rows = slice(start, start + chunk)
        scores = scores_of(keys[...], queries[rows], bias_ref[:, rows], scale)
        top = jnp.max(scores, axis=0, keepdims=True)
        weights = jnp.exp(scores - top)
        total = 1.0 / jnp.sum(weights, axis=0, keepdims=True)
        probs_low = (weights * total).astype(jnp.bfloat16)
        heads[rows] = dot(value_cols, probs_low, NN).T.astype(jnp.bfloat16)
        top_ref[:, rows] = top
        sum_ref[:, rows] = total
    size = outs[0].shape[0]
    for mask, out in enumerate(outs):
        out[...] = heads[pl.ds(pl.multiple_of(((ids[0] >> 1) ^ mask) * size, size), size)]


def forward(ids, bias, parts, scale):
    peers, tokens = len(parts), bias.shape[1]
    quads = peers // 2
    return pl.pallas_call(
        functools.partial(forward_kernel, peers, 2 * tokens // peers, scale),
        out_shape=[struct(2 * tokens // peers, HD)] * quads
        + [struct(1, tokens, dtype=jnp.float32)] * 2,
        in_specs=[pl.BlockSpec(memory_space=pltpu.SMEM)] + whole(peers + 1),
        out_specs=whole(quads + 2),
        scratch_shapes=[pltpu.VMEM((tokens, HD), jnp.bfloat16)] * 4,
        compiler_params=params(24),
        cost_estimate=cost(16 * tokens * tokens * HD, 4 * tokens * HD * 2),
        name="attend",
    )(ids, bias, *parts)


def backward_kernel(peers, chunk, scale, ids, bias_ref, top_ref, sum_ref, *refs):
    parts, refs = refs[:peers], refs[peers:]
    grad_parts, refs = refs[:peers], refs[peers:]
    outs, refs = refs[:peers], refs[peers:]
    keys, values, queries, grads, query_grad, key_sum, value_sum = refs
    rows_each = grad_parts[0].shape[0]
    load_heads(ids, parts, rows_each, keys, values, queries)
    load_heads(ids, grad_parts, rows_each, grads)
    key_cols = keys[...].T
    for start in range(0, keys.shape[0], chunk):
        rows = slice(start, start + chunk)
        scores = scores_of(keys[...], queries[rows], bias_ref[:, rows], scale)
        probs = jnp.exp(scores - top_ref[:, rows]) * sum_ref[:, rows]
        prob_grad = dot(values[...], grads[rows], NT)
        delta = jnp.sum(probs * prob_grad, axis=0, keepdims=True)
        score_grad = (probs * (prob_grad - delta)).astype(jnp.bfloat16)
        value_part = dot(probs.astype(jnp.bfloat16), grads[rows], NN)
        key_part = dot(score_grad, queries[rows], NN)
        if start == 0:
            value_sum[...] = value_part
            key_sum[...] = key_part
        else:
            value_sum[...] += value_part
            key_sum[...] += key_part
        query_grad[rows] = (dot(key_cols, score_grad, NN) * scale).T.astype(jnp.bfloat16)
    for mask, out in enumerate(outs):
        place = pl.ds(pl.multiple_of((ids[0] ^ mask) * rows_each, rows_each), rows_each)
        out[:rows_each] = query_grad[place]
        out[rows_each : 2 * rows_each] = (key_sum[place] * scale).astype(jnp.bfloat16)
        out[2 * rows_each :] = value_sum[place].astype(jnp.bfloat16)


def backward(ids, bias, top, total, parts, grad_parts, scale):
    peers, tokens = len(parts), bias.shape[1]
    return pl.pallas_call(
        functools.partial(backward_kernel, peers, 2 * tokens // peers, scale),
        out_shape=[struct(3 * tokens // peers, HD)] * peers,
        in_specs=[pl.BlockSpec(memory_space=pltpu.SMEM)] + whole(2 * peers + 3),
        out_specs=whole(peers),
        scratch_shapes=[pltpu.VMEM((tokens, HD), jnp.bfloat16)] * 5
        + [pltpu.VMEM((tokens, HD), jnp.float32)] * 2,
        compiler_params=params(24),
        cost_estimate=cost(40 * tokens * tokens * HD, 8 * tokens * HD * 2),
        name="attend_back",
    )(ids, bias, top, total, *parts, *grad_parts)


def unpack_kernel(ids, *refs):
    parts, targets = refs[:-3], refs[-3:]
    for mask, part in enumerate(parts):
        columns = pl.ds(pl.multiple_of((ids[0] ^ mask) * HD, HD), HD)
        rows = targets[0].shape[0]
        for index, target in enumerate(targets):
            target[:, columns] = part[index * rows : (index + 1) * rows]


def unpack(ids, parts):
    rows = parts[0].shape[0] // 3
    return pl.pallas_call(
        unpack_kernel,
        out_shape=[struct(rows, HD * len(parts))] * 3,
        in_specs=[pl.BlockSpec(memory_space=pltpu.SMEM)] + whole(len(parts)),
        out_specs=whole(3),
        compiler_params=params(16),
        name="unpack_grads",
    )(ids, *parts)


def project_kernel(quads, ids, near, far, weight_ref, out_ref, attended):
    rows = out_ref.shape[0]

    @pl.when(pl.program_id(0) == 0)
    def _():
        side = ids[0] & 1
        for mask in range(quads):
            pair = ((ids[0] >> 1) ^ mask) * 2
            mine = pl.ds(pl.multiple_of((2 * mask + side) * rows, rows), rows)
            for head, block in (
                (pair + side, near[mine]),
                (pair + 1 - side, far[mask * rows : (mask + 1) * rows]),
            ):
                attended[:, pl.ds(pl.multiple_of(head * HD, HD), HD)] = block

    out_ref[...] = dot(attended[...], weight_ref[...], NN).astype(jnp.bfloat16)


def project(ids, near, far, out_weight, quads):
    rows = far.shape[0] // quads
    depth, width = out_weight.shape
    tile = width // 4
    grid = pltpu.PrefetchScalarGridSpec(
        num_scalar_prefetch=1,
        grid=(width // tile,),
        in_specs=[
            pl.BlockSpec(near.shape, lambda i, ids: (0, 0)),
            pl.BlockSpec(far.shape, lambda i, ids: (0, 0)),
            pl.BlockSpec((depth, tile), lambda i, ids: (0, i)),
        ],
        out_specs=pl.BlockSpec((rows, tile), lambda i, ids: (0, i)),
        scratch_shapes=[pltpu.VMEM((rows, depth), jnp.bfloat16)],
    )
    return pl.pallas_call(
        functools.partial(project_kernel, quads),
        out_shape=struct(rows, width),
        grid_spec=grid,
        compiler_params=params(16),
        cost_estimate=cost(2 * rows * depth * width, depth * width * 2),
        name="project",
    )(ids, near, far, out_weight)


def stack_pair_kernel(ids, *refs):
    blocks, (near, far) = refs[:-2], refs[-2:]
    rows = blocks[0].shape[0] // 2
    for mask, block in enumerate(blocks):
        near[2 * mask * rows : 2 * (mask + 1) * rows] = block[...]
        theirs = pl.ds(pl.multiple_of((1 - (ids[0] & 1)) * rows, rows), rows)
        far[mask * rows : (mask + 1) * rows] = block[theirs]


def stack_pair(ids, blocks):
    rows = len(blocks) * blocks[0].shape[0]
    return pl.pallas_call(
        stack_pair_kernel,
        out_shape=[struct(rows, HD), struct(rows // 2, HD)],
        in_specs=[pl.BlockSpec(memory_space=pltpu.SMEM)] + whole(len(blocks)),
        out_specs=whole(2),
        compiler_params=params(8),
        name="stack_pair",
    )(ids, *blocks)


def weight_part_kernel(quads, ids, *refs):
    docs = len(refs) - quads - 2
    heads, grads, outs = refs[:docs], refs[docs : docs + 2], refs[docs + 2 :]
    rows = heads[0].shape[0] // (2 * quads)
    right = jnp.concatenate([grad[...] for grad in grads], axis=0)
    side = ids[0] & 1
    for mask, out in enumerate(outs):
        places = [
            pl.ds(pl.multiple_of((2 * mask + index) * rows, rows), rows) for index in (side, 1 - side)
        ]
        left = jnp.concatenate([head[place] for place in places for head in heads], axis=0)
        out[...] = dot(left, right, TN).astype(jnp.bfloat16)


def weight_parts(ids, heads, grads, quads):
    width = grads[0].shape[1]
    return pl.pallas_call(
        functools.partial(weight_part_kernel, quads),
        out_shape=[struct(HD, width)] * quads,
        in_specs=[pl.BlockSpec(memory_space=pltpu.SMEM)] + whole(len(heads) + 2),
        out_specs=whole(quads),
        compiler_params=params(16),
        cost_estimate=cost(4 * quads * HD * width * grads[0].shape[0], 4 << 20),
        name="weight_part",
    )(ids, *heads, *grads)


def weight_sum_kernel(factor, *refs):
    total = refs[0][...].astype(jnp.float32)
    for part in refs[1:-1]:
        total += part[...].astype(jnp.float32)
    refs[-1][...] = (total * factor).astype(jnp.bfloat16)


def weight_sum(parts, factor):
    return pl.pallas_call(
        functools.partial(weight_sum_kernel, factor),
        out_shape=struct(*parts[0].shape),
        in_specs=whole(len(parts)),
        out_specs=pl.BlockSpec(memory_space=VMEM),
        compiler_params=params(8),
        name="weight_sum",
    )(*parts)


def weight_join_kernel(ids, *refs):
    width = refs[0].shape[1]
    for mask, part in enumerate(refs[:-1]):
        columns = pl.ds(pl.multiple_of((ids[1] ^ mask) * width, width), width)
        refs[-1][:, columns] = part[...].astype(jnp.float32)


def weight_join(ids, parts):
    rows, width = parts[0].shape
    return pl.pallas_call(
        weight_join_kernel,
        out_shape=struct(rows, width * len(parts), dtype=jnp.float32),
        in_specs=[pl.BlockSpec(memory_space=pltpu.SMEM)] + whole(len(parts)),
        out_specs=pl.BlockSpec(memory_space=VMEM),
        compiler_params=params(8),
        name="weight_join",
    )(ids, *parts)


def gather_rep(block):
    blocks, bit = [block], 1
    while bit < lax.axis_size("rep"):
        blocks = blocks + [swap(item, "rep", bit) for item in blocks]
        bit *= 2
    return blocks


def dense_bias(pattern, tokens):
    blocks = pattern.shape[0]
    named = pattern[:, :, None] == jnp.arange(blocks, dtype=pattern.dtype)
    counts = jnp.sum(named.astype(jnp.float32), axis=1).T
    bias = jnp.where(counts > 0, jnp.log(jnp.maximum(counts, 1.0)), MASKED)
    return jnp.repeat(bias, tokens // blocks, axis=1)


def dense_local(query_in, key_in, value_in, out_weight, grad_out, pattern):
    seq_count, rep_count = lax.axis_size("seq"), lax.axis_size("rep")
    tokens_here = query_in.shape[1]
    tokens = tokens_here * seq_count
    quads = seq_count // 2
    scale = 1.0 / math.sqrt(HD)
    ids = jnp.stack([lax.axis_index("seq"), lax.axis_index("rep")]).astype(jnp.int32)
    bias = dense_bias(pattern, tokens)

    sends = pack(ids, key_in[0], value_in[0], query_in[0], seq_count)
    parts = [sends[0]] + [swap(sends[mask], "seq", mask) for mask in range(1, seq_count)]
    grad_sends = head_grads(ids, grad_out[0], out_weight, seq_count)
    grad_parts = [grad_sends[0]] + [swap(grad_sends[mask], "seq", mask) for mask in range(1, seq_count)]
    grad_quarters = quarters(ids, grad_out[0], rep_count)
    doc_grads = jnp.concatenate(
        [grad_quarters[0]] + [swap(grad_quarters[mask], "rep", mask) for mask in range(1, rep_count)],
        axis=0,
    )
    pair_grads = swap(doc_grads, "seq", 1)

    *heads, top, total = forward(ids, bias, parts, scale)
    near = [heads[0]] + [swap(heads[mask], "seq", 2 * mask) for mask in range(1, quads)]
    back = backward(ids, bias, top, total, parts, grad_parts, scale)

    near, far_send = stack_pair(ids, near)
    far = swap(far_send, "seq", 1)
    mixed_out = project(ids, near, far, out_weight, quads)

    weight_sends = weight_parts(ids, gather_rep(near), [doc_grads, pair_grads], quads)
    weight_blocks = [weight_sends[0]] + [
        swap(weight_sends[mask], "seq", 2 * mask) for mask in range(1, quads)
    ]
    factor = 1.0 / math.sqrt(rep_count * tokens)
    weight_grad = weight_join(ids, gather_rep(weight_sum(weight_blocks, factor)))

    returned = [back[0]] + [swap(back[mask], "seq", mask) for mask in range(1, seq_count)]
    query_grad, key_grad, value_grad = unpack(ids, returned)
    return (mixed_out[None], query_grad[None], key_grad[None], value_grad[None], weight_grad)


def local(query_in, key_in, value_in, out_weight, grad_out, pattern):
    seq_count, rep_count = lax.axis_size("seq"), lax.axis_size("rep")
    one_head_each = seq_count * HD == query_in.shape[2]
    paired = seq_count & (seq_count - 1) == 0 and rep_count & (rep_count - 1) == 0 and seq_count > 1
    if one_head_each and paired and query_in.shape[0] == 1:
        return dense_local(query_in, key_in, value_in, out_weight, grad_out, pattern)
    return general_local(query_in, key_in, value_in, out_weight, grad_out, pattern)


def general_local(query_in, key_in, value_in, out_weight, grad_out, pattern):
    seq_count = lax.axis_size("seq")
    rep_count = lax.axis_size("rep")
    tokens_here = query_in.shape[1]
    width = query_in.shape[2]
    head_size = HD
    head_count = width // head_size
    groups = max(seq_count // head_count, 1)
    per_device = max(head_count // seq_count, 1)
    head_groups = head_count // per_device
    local_blocks = tokens_here // BLK
    group_rows = BLK // groups
    all_blocks = seq_count * local_blocks
    columns = per_device * head_size
    span = pattern.shape[1]
    block_run = math.gcd(all_blocks, 32)
    run_count = all_blocks // block_run
    scale = 1.0 / math.sqrt(head_size)

    def to_heads(source):
        shaped = source.reshape(local_blocks, groups, group_rows, head_groups, columns)
        return shaped.transpose(3, 1, 0, 2, 4).reshape(
            seq_count, local_blocks * group_rows, columns
        )

    def to_tokens(source):
        shaped = source.reshape(head_groups, groups, local_blocks, group_rows, columns)
        return shaped.transpose(2, 1, 3, 0, 4).reshape(tokens_here, width)

    query_local = query_in[0]
    key_local = key_in[0]
    value_local = value_in[0]
    grad_local = grad_out[0]

    def spread(source):
        grouped = source.reshape(tokens_here, head_groups, columns).transpose(1, 0, 2)
        copies = jnp.broadcast_to(grouped[:, None], (head_groups, groups, tokens_here, columns))
        return copies.reshape(seq_count, tokens_here, columns)

    query_heads, key_all, value_all = (
        lax.all_to_all(to_heads(query_local), "seq", split_axis=0, concat_axis=0, tiled=True),
        lax.all_to_all(spread(key_local), "seq", split_axis=0, concat_axis=0, tiled=True),
        lax.all_to_all(spread(value_local), "seq", split_axis=0, concat_axis=0, tiled=True),
    )
    attended_grad = lax.dot_general(
        grad_local, out_weight, (((1,), (1,)), ((), ())), preferred_element_type=jnp.float32
    ).astype(jnp.bfloat16)
    grad_heads = lax.all_to_all(
        to_heads(attended_grad), "seq", split_axis=0, concat_axis=0, tiled=True
    )
    key_blocks = key_all.reshape(all_blocks, BLK, per_device, head_size)
    value_blocks = value_all.reshape(all_blocks, BLK, per_device, head_size)
    query_runs = query_heads.reshape(run_count, block_run, group_rows, per_device, head_size)
    grad_runs = grad_heads.reshape(run_count, block_run, group_rows, per_device, head_size)
    pattern_runs = pattern.reshape(run_count, block_run, span)

    def attend_step(carry, items):
        key_acc, value_acc = carry
        query_run, grad_run, pattern_run = items
        key_gathered = key_blocks[pattern_run].reshape(block_run, span * BLK, per_device, head_size)
        value_gathered = value_blocks[pattern_run].reshape(
            block_run, span * BLK, per_device, head_size
        )
        scores = (
            jnp.einsum(
                "crhd,ckhd->chrk", query_run, key_gathered, preferred_element_type=jnp.float32
            )
            * scale
        )
        shifted = scores - jnp.max(scores, axis=-1, keepdims=True)
        weights = jnp.exp(shifted)
        probs = weights / jnp.sum(weights, axis=-1, keepdims=True)
        probs_low = probs.astype(jnp.bfloat16)
        result = jnp.einsum(
            "chrk,ckhd->crhd", probs_low, value_gathered, preferred_element_type=jnp.float32
        ).astype(jnp.bfloat16)
        prob_grad = jnp.einsum(
            "crhd,ckhd->chrk", grad_run, value_gathered, preferred_element_type=jnp.float32
        )
        delta = jnp.sum(probs * prob_grad, axis=-1, keepdims=True)
        score_grad = (probs * (prob_grad - delta)).astype(jnp.bfloat16)
        query_part = (
            jnp.einsum(
                "chrk,ckhd->crhd", score_grad, key_gathered, preferred_element_type=jnp.float32
            )
            * scale
        ).astype(jnp.bfloat16)
        key_contrib = (
            jnp.einsum("chrk,crhd->ckhd", score_grad, query_run, preferred_element_type=jnp.float32)
            * scale
        )
        value_contrib = jnp.einsum(
            "chrk,crhd->ckhd", probs_low, grad_run, preferred_element_type=jnp.float32
        )
        key_acc = key_acc.at[pattern_run].add(
            key_contrib.reshape(block_run, span, BLK, per_device, head_size)
        )
        value_acc = value_acc.at[pattern_run].add(
            value_contrib.reshape(block_run, span, BLK, per_device, head_size)
        )
        return ((key_acc, value_acc), (result, query_part))

    zero_grads = jnp.zeros((all_blocks, BLK, per_device, head_size), jnp.float32)
    (key_acc, value_acc), (out_heads, query_parts) = lax.scan(
        attend_step, (zero_grads, zero_grads), (query_runs, grad_runs, pattern_runs)
    )
    out_send = out_heads.reshape(seq_count, local_blocks * group_rows, columns)
    attended = to_tokens(lax.all_to_all(out_send, "seq", split_axis=0, concat_axis=0, tiled=True))
    mixed_out = jnp.dot(attended, out_weight, preferred_element_type=jnp.float32).astype(
        jnp.bfloat16
    )
    norm_factor = 1.0 / math.sqrt(rep_count * seq_count * tokens_here)
    weight_shard = lax.psum_scatter(
        lax.dot_general(
            attended, grad_local, (((0,), (0,)), ((), ())), preferred_element_type=jnp.float32
        ),
        ("seq", "rep"),
        scatter_dimension=0,
        tiled=True,
    )
    weight_grad = lax.all_gather(
        (weight_shard * norm_factor).astype(jnp.bfloat16), "rep", axis=0, tiled=True
    ).astype(jnp.float32)
    query_send = query_parts.reshape(seq_count, local_blocks * group_rows, columns)
    key_send = key_acc.astype(jnp.bfloat16).reshape(seq_count, tokens_here, columns)
    value_send = value_acc.astype(jnp.bfloat16).reshape(seq_count, tokens_here, columns)
    query_back, key_back, value_back = (
        lax.all_to_all(query_send, "seq", split_axis=0, concat_axis=0, tiled=True),
        lax.all_to_all(key_send, "seq", split_axis=0, concat_axis=0, tiled=True),
        lax.all_to_all(value_send, "seq", split_axis=0, concat_axis=0, tiled=True),
    )

    def fold_groups(source):
        summed = jnp.sum(
            source.reshape(head_groups, groups, tokens_here, columns).astype(jnp.float32), axis=1
        )
        return summed.astype(jnp.bfloat16).transpose(1, 0, 2).reshape(tokens_here, width)

    query_grad = to_tokens(query_back)
    key_grad = fold_groups(key_back)
    value_grad = fold_groups(value_back)
    return (mixed_out[None], query_grad[None], key_grad[None], value_grad[None], weight_grad)


def solution(mesh):
    placed = (
        P("rep", "seq", None),
        P("rep", "seq", None),
        P("rep", "seq", None),
        P(),
        P("rep", "seq", None),
        P(),
    )
    return jax.shard_map(
        local,
        mesh=mesh,
        in_specs=placed,
        out_specs=(
            P("rep", "seq", None),
            P("rep", "seq", None),
            P("rep", "seq", None),
            P("rep", "seq", None),
            P("seq", None),
        ),
        check_vma=False,
    )
```

```python
import functools
import math

import jax
import jax.numpy as jnp
from jax import lax
from jax.experimental import pallas as pl
from jax.experimental.pallas import tpu as pltpu
from jax.sharding import PartitionSpec as P

HD = 128
BLK = 64
MASKED = -1e30
VMEM = pltpu.VMEM
ANY_SPEC = pl.BlockSpec(memory_space=pl.ANY)
VMEM_SPEC = pl.BlockSpec()
NT = (((1,), (1,)), ((), ()))
NN = (((1,), (0,)), ((), ()))
TN = (((0,), (0,)), ((), ()))
WIDE = 58
PROJECT_FLOPS = 4 << 30
JOIN_FLOPS = 2 << 30


def dot(left, right, dims):
    return lax.dot_general(left, right, dims, preferred_element_type=jnp.float32)


def params(mib):
    return pltpu.CompilerParams(vmem_limit_bytes=mib * 1024 * 1024)


def cost(flops=1, moved=1):
    return pl.CostEstimate(flops=flops, bytes_accessed=moved, transcendentals=0)


def struct(*shape, dtype=jnp.bfloat16):
    return jax.ShapeDtypeStruct(shape, dtype)


def span(index, size):
    return pl.ds(pl.multiple_of(index * size, size), size)


def swap(array, axis, mask):
    return lax.ppermute(array, axis, [(i, i ^ mask) for i in range(lax.axis_size(axis))])


def gather_rep(block):
    blocks, bit = {0: block}, lax.axis_size("rep") // 2
    while bit:
        blocks |= {mask | bit: swap(item, "rep", bit) for mask, item in blocks.items()}
        bit //= 2
    return [blocks[mask] for mask in sorted(blocks)]


def after(*arrays):
    return lax.optimization_barrier(arrays)


def anchored(kernel):
    return lambda anchor, *refs: kernel(*refs)


def members_of(peers):
    return peers // 2


def member(mask=0):
    return (lax.axis_index("seq") ^ mask) & (members_of(lax.axis_size("seq")) - 1)


def half_of():
    return lax.axis_index("seq") // members_of(lax.axis_size("seq"))


def pack_kernel(key_ref, value_ref, send, *refs):
    held, sem = refs[:2], refs[2]
    rows, width = key_ref.shape
    peers = send.shape[0]
    loads = [
        pltpu.make_async_copy(source, target, sem.at[index])
        for index, (source, target) in enumerate(zip((key_ref, value_ref), held))
    ]
    for load in loads:
        load.start()
    for index, source in enumerate(held):
        loads[index].wait()
        for peer in range(peers):
            for slot in range(2):
                head = peer % members_of(peers) + slot * members_of(peers)
                place = pl.ds((2 * index + slot) * rows, rows)
                send[peer, place] = source[:, head * HD : (head + 1) * HD]


def pack(keys, values, peers):
    rows, width = keys.shape
    return pl.pallas_call(
        pack_kernel,
        out_shape=struct(peers, 4 * rows, HD),
        in_specs=[ANY_SPEC] * 2,
        out_specs=VMEM_SPEC,
        scratch_shapes=[VMEM((rows, width), jnp.bfloat16)] * 2 + [pltpu.SemaphoreType.DMA((2,))],
        compiler_params=params(WIDE),
        cost_estimate=cost(),
        name="pack_keys",
    )(keys, values)


def head_grad_kernel(query_ref, grad_ref, weight_ref, *refs):
    sends, (query, grad, weight, head_grad, sem) = refs[:-5], refs[-5:]
    rows = query_ref.shape[0]
    members = len(sends)
    loads = [
        pltpu.make_async_copy(source, target, sem.at[index])
        for index, (source, target) in enumerate(
            zip((query_ref, grad_ref, weight_ref), (query, grad, weight))
        )
    ]
    for load in loads:
        load.start()
    loads[0].wait()
    for mask, send in enumerate(sends):
        for slot in range(2):
            send[slot * rows : (slot + 1) * rows] = query[:, span(member(mask) + slot * members, HD)]
    loads[1].wait()
    loads[2].wait()
    head_grad[...] = dot(weight[...], grad[...], NT).astype(jnp.bfloat16)
    for mask, send in enumerate(sends):
        for slot in range(2):
            place = pl.ds(2 * rows + slot * HD, HD)
            send[place] = head_grad[span(member(mask) + slot * members, HD)]


def head_grads(queries, grads, out_weight, members):
    rows, width = queries.shape
    return pl.pallas_call(
        head_grad_kernel,
        out_shape=[struct(2 * rows + 2 * HD, HD)] * members,
        in_specs=[ANY_SPEC] * 3,
        out_specs=[VMEM_SPEC] * members,
        scratch_shapes=[
            VMEM(queries.shape, jnp.bfloat16),
            VMEM(grads.shape, jnp.bfloat16),
            VMEM(out_weight.shape, jnp.bfloat16),
            VMEM((width, rows), jnp.bfloat16),
            pltpu.SemaphoreType.DMA((3,)),
        ],
        compiler_params=params(24),
        cost_estimate=cost(),
        name="head_grads",
    )(queries, grads, out_weight)


def join_queries_kernel(*refs):
    parts, (queries, grads) = refs[:-2], refs[-2:]
    rows = parts[0].shape[0] // 4
    for mask, part in enumerate(parts):
        for slot in range(2):
            queries[slot, span(member(mask), rows)] = part[slot * rows : (slot + 1) * rows]
            grad = part[2 * rows + slot * HD : 2 * rows + (slot + 1) * HD]
            grads[slot, :, span(member(mask), rows)] = grad


def join_queries(parts):
    tokens = len(parts) * parts[0].shape[0] // 4
    return pl.pallas_call(
        join_queries_kernel,
        out_shape=[struct(2, tokens, HD), struct(2, HD, tokens)],
        in_specs=[VMEM_SPEC] * len(parts),
        out_specs=[VMEM_SPEC] * 2,
        compiler_params=params(8),
        cost_estimate=cost(JOIN_FLOPS),
        name="join_queries",
    )(*parts)


def load_heads(pairs, keys, values):
    rows = pairs.shape[1] // 4
    for peer in range(pairs.shape[0]):
        for slot in range(2):
            place = slice(peer * rows, (peer + 1) * rows)
            keys[slot, place] = pairs[peer, slot * rows : (slot + 1) * rows]
            values[slot, place] = pairs[peer, (2 + slot) * rows : (3 + slot) * rows]


def scores_of(keys, queries, bias, scale):
    blocks = bias.shape[0]
    scores = dot(keys, queries, NT) * scale
    shaped = scores.reshape(blocks, BLK, queries.shape[0]) + bias[:, None, :]
    return shaped.reshape(scores.shape)


def forward_kernel(chunk, scale, bias_ref, pairs, queries, near, top_ref, sum_ref, keys, values):
    load_heads(pairs, keys, values)
    tokens = queries.shape[1]
    for slot in range(2):
        value_cols = values[slot].T
        for step in range(tokens // chunk):
            rows = slice(step * chunk, (step + 1) * chunk)
            bias = bias_ref[:, span(half_of() * (tokens // chunk) + step, chunk)]
            scores = scores_of(keys[slot], queries[slot, rows], bias, scale)
            top = jnp.max(scores, axis=0, keepdims=True)
            weights = jnp.exp(scores - top)
            total = 1.0 / jnp.sum(weights, axis=0, keepdims=True)
            probs_low = (weights * total).astype(jnp.bfloat16)
            place = pl.ds(slot * tokens + step * chunk, chunk)
            near[place] = dot(value_cols, probs_low, NN).T.astype(jnp.bfloat16)
            top_ref[slot : slot + 1, rows] = top
            sum_ref[slot : slot + 1, rows] = total


def forward(bias, pairs, queries, scale):
    tokens = bias.shape[1]
    chunk = 2 * tokens // pairs.shape[0]
    stats = struct(2, tokens // 2, dtype=jnp.float32)
    return pl.pallas_call(
        functools.partial(forward_kernel, chunk, scale),
        out_shape=[struct(tokens, HD), stats, stats],
        in_specs=[VMEM_SPEC] * 3,
        out_specs=[VMEM_SPEC] * 3,
        scratch_shapes=[VMEM((2, tokens, HD), jnp.bfloat16)] * 2,
        compiler_params=params(24),
        cost_estimate=cost(),
        name="attend",
    )(bias, pairs, queries)


def backward_kernel(chunk, scale, bias_ref, top_ref, sum_ref, pairs, queries, grads, near, *refs):
    returns, outs, (keys, values, query_grad, key_sum, value_sum) = refs[0], refs[1:-5], refs[-5:]
    load_heads(pairs, keys, values)
    tokens = queries.shape[1]
    peers = returns.shape[0]
    here = returns.shape[1] // 4
    for slot in range(2):
        key_cols = keys[slot].T
        for step in range(tokens // chunk):
            rows = slice(step * chunk, (step + 1) * chunk)
            bias = bias_ref[:, span(half_of() * (tokens // chunk) + step, chunk)]
            scores = scores_of(keys[slot], queries[slot, rows], bias, scale)
            probs = jnp.exp(scores - top_ref[slot : slot + 1, rows]) * sum_ref[slot : slot + 1, rows]
            prob_grad = dot(values[slot], grads[slot, :, rows], NN)
            delta = jnp.sum(probs * prob_grad, axis=0, keepdims=True)
            score_grad = (probs * (prob_grad - delta)).astype(jnp.bfloat16)
            value_part = dot(probs.astype(jnp.bfloat16), grads[slot, :, rows], NT)
            key_part = dot(score_grad, queries[slot, rows], NN)
            if step == 0:
                value_sum[...] = value_part
                key_sum[...] = key_part
            else:
                value_sum[...] += value_part
                key_sum[...] += key_part
            query_part = dot(key_cols, score_grad, NN) * scale
            query_grad[slot, rows] = query_part.T.astype(jnp.bfloat16)
        for peer in range(peers):
            place = slice(peer * here, (peer + 1) * here)
            key_low = (key_sum[place] * scale).astype(jnp.bfloat16)
            returns[peer, slot * here : (slot + 1) * here] = key_low
            value_low = value_sum[place].astype(jnp.bfloat16)
            returns[peer, (2 + slot) * here : (3 + slot) * here] = value_low
        for mask, out in enumerate(outs):
            theirs = span(member(mask), here)
            out[slot * here : (slot + 1) * here] = query_grad[slot, theirs]
            theirs = span(slot * len(outs) + member(mask), here)
            out[(2 + slot) * here : (3 + slot) * here] = near[theirs]


def backward(bias, top, total, pairs, queries, grads, near, scale):
    peers, tokens = pairs.shape[0], bias.shape[1]
    members = members_of(peers)
    here = tokens // peers
    return pl.pallas_call(
        functools.partial(backward_kernel, 2 * here, scale),
        out_shape=[struct(peers, 4 * here, HD)] + [struct(4 * here, HD)] * members,
        in_specs=[VMEM_SPEC] * 7,
        out_specs=[VMEM_SPEC] * (1 + members),
        scratch_shapes=[VMEM((2, tokens, HD), jnp.bfloat16)] * 2
        + [VMEM((2, tokens // 2, HD), jnp.bfloat16)]
        + [VMEM((tokens, HD), jnp.float32)] * 2,
        compiler_params=params(24),
        cost_estimate=cost(),
        name="attend_back",
    )(bias, top, total, pairs, queries, grads, near)


def unpack_kernel(returned, *refs):
    queries, (query_grad, key_grad, value_grad, token) = refs[:-4], refs[-4:]
    token[...] = jnp.zeros_like(token)
    members = len(queries)
    here = query_grad.shape[0]
    for index in range(members):
        for slot in range(2):
            columns = pl.ds((index + slot * members) * HD, HD)
            for target, first in ((key_grad, slot), (value_grad, 2 + slot)):
                rows = slice(first * here, (first + 1) * here)
                both = returned[index, rows].astype(jnp.float32) + returned[
                    index + members, rows
                ].astype(jnp.float32)
                target[:, columns] = both.astype(jnp.bfloat16)
            part = queries[index][slot * here : (slot + 1) * here]
            query_grad[:, span(member(index) + slot * members, HD)] = part


def unpack(returned, queries, rows, width):
    return pl.pallas_call(
        unpack_kernel,
        out_shape=[struct(rows, width)] * 3 + [struct(16, HD)],
        in_specs=[VMEM_SPEC] * (1 + len(queries)),
        out_specs=[VMEM_SPEC] * 4,
        compiler_params=params(16),
        cost_estimate=cost(1, 24 * rows * width),
        name="unpack_grads",
    )(returned, *queries)


def project_kernel(*refs):
    parts, (weight_ref, out_ref, token, attended) = refs[:-4], refs[-4:]
    token[...] = jnp.zeros_like(token)
    rows = out_ref.shape[0]

    @pl.when(pl.program_id(0) == 0)
    def _():
        for mask, part in enumerate(parts):
            for slot in range(2):
                columns = span(member(mask) + slot * len(parts), HD)
                attended[:, columns] = part[(2 + slot) * rows : (3 + slot) * rows]

    out_ref[...] = dot(attended[...], weight_ref[...], NN).astype(jnp.bfloat16)


def project(parts, out_weight):
    rows = parts[0].shape[0] // 4
    depth, width = out_weight.shape
    tile = width // 4
    return pl.pallas_call(
        project_kernel,
        out_shape=[struct(rows, width), struct(16, HD)],
        grid=(width // tile,),
        in_specs=[pl.BlockSpec(part.shape, lambda i: (0, 0)) for part in parts]
        + [pl.BlockSpec((depth, tile), lambda i: (0, i))],
        out_specs=[
            pl.BlockSpec((rows, tile), lambda i: (0, i)),
            pl.BlockSpec((16, HD), lambda i: (0, 0)),
        ],
        scratch_shapes=[VMEM((rows, depth), jnp.bfloat16)],
        compiler_params=params(24),
        cost_estimate=cost(PROJECT_FLOPS, 1),
        name="project",
    )(*parts, out_weight)


def weight_part_kernel(docs, near, *refs):
    grads, (own, send) = refs[:-2], refs[-2:]
    members = len(grads)
    rows = grads[0].shape[0]
    width = grads[0].shape[1] // docs
    lefts = []
    for slot in range(2):
        places = [span(slot * members + member(mask), rows) for mask in range(members)]
        lefts.append(jnp.concatenate([near[place] for place in places], axis=0).T)
    for mask in range(docs):
        columns = span(lax.axis_index("rep") ^ mask, width)
        right = jnp.concatenate([grad[:, columns] for grad in grads], axis=0)
        for slot, left in enumerate(lefts):
            place = pl.ds((mask // 2 * 2 + slot) * HD, HD)
            if mask % 2:
                send[place] = dot(left, right, NN).astype(jnp.bfloat16)
            else:
                own[place] = dot(left, right, NN)


def weight_parts(near, grads, docs):
    width = grads[0].shape[1] // docs
    return pl.pallas_call(
        functools.partial(weight_part_kernel, docs),
        out_shape=[
            struct(docs * HD, width, dtype=jnp.float32),
            struct(docs * HD, width),
        ],
        in_specs=[VMEM_SPEC] * (1 + len(grads)),
        out_specs=[VMEM_SPEC] * 2,
        compiler_params=params(24),
        cost_estimate=cost(),
        name="weight_part",
    )(near, *grads)


def weight_fold_kernel(own, other, keep, send):
    rows = keep.shape[0]
    keep[...] = own[:rows] + other[:rows].astype(jnp.float32)
    send[...] = (own[rows:] + other[rows:].astype(jnp.float32)).astype(jnp.bfloat16)


def weight_fold(own, other):
    rows, width = own.shape
    return pl.pallas_call(
        weight_fold_kernel,
        out_shape=[struct(rows // 2, width, dtype=jnp.float32), struct(rows // 2, width)],
        in_specs=[VMEM_SPEC] * 2,
        out_specs=[VMEM_SPEC] * 2,
        compiler_params=params(8),
        cost_estimate=cost(),
        name="weight_fold",
    )(own, other)


def weight_split_kernel(own, other, keep, send):
    lower = half_of() == 0
    rows = keep.shape[0]
    first = own[:rows] + other[:rows].astype(jnp.float32)
    second = own[rows:] + other[rows:].astype(jnp.float32)
    keep[...] = jnp.where(lower, first, second)
    send[...] = jnp.where(lower, second, first).astype(jnp.bfloat16)


def weight_split(own, other):
    rows, width = own.shape
    return pl.pallas_call(
        weight_split_kernel,
        out_shape=[struct(rows // 2, width, dtype=jnp.float32), struct(rows // 2, width)],
        in_specs=[VMEM_SPEC] * 2,
        out_specs=[VMEM_SPEC] * 2,
        compiler_params=params(8),
        cost_estimate=cost(),
        name="weight_split",
    )(own, other)


def weight_sum_kernel(factor, own, other, total):
    total[...] = ((own[...] + other[...].astype(jnp.float32)) * factor).astype(jnp.bfloat16)


def weight_sum(anchor, own, other, factor):
    return pl.pallas_call(
        anchored(functools.partial(weight_sum_kernel, factor)),
        out_shape=struct(*own.shape),
        in_specs=[ANY_SPEC] + [VMEM_SPEC] * 2,
        out_specs=VMEM_SPEC,
        compiler_params=params(8),
        cost_estimate=cost(),
        name="weight_sum",
    )(anchor, own, other)


def weight_join_kernel(*refs):
    width = refs[0].shape[1]
    for mask, part in enumerate(refs[:-1]):
        refs[-1][:, span(lax.axis_index("rep") ^ mask, width)] = part[...].astype(jnp.float32)


def weight_join(parts):
    rows, width = parts[0].shape
    return pl.pallas_call(
        weight_join_kernel,
        out_shape=struct(rows, width * len(parts), dtype=jnp.float32),
        in_specs=[VMEM_SPEC] * len(parts),
        out_specs=VMEM_SPEC,
        compiler_params=params(8),
        cost_estimate=cost(),
        name="weight_join",
    )(*parts)


def dense_bias(pattern, tokens):
    blocks = pattern.shape[0]
    named = pattern[:, :, None] == jnp.arange(blocks, dtype=pattern.dtype)
    counts = jnp.sum(named.astype(jnp.float32), axis=1).T
    bias = jnp.where(counts > 0, jnp.log(jnp.maximum(counts, 1.0)), MASKED)
    return jnp.repeat(bias, tokens // blocks, axis=1)


def dense_local(query_in, key_in, value_in, out_weight, grad_out, pattern):
    seq_count, rep_count = lax.axis_size("seq"), lax.axis_size("rep")
    tokens_here = query_in.shape[1]
    tokens = tokens_here * seq_count
    members = members_of(seq_count)
    scale = 1.0 / math.sqrt(HD)
    bias = dense_bias(pattern, tokens)

    pairs = lax.all_to_all(
        pack(key_in[0], value_in[0], seq_count), "seq", split_axis=0, concat_axis=0, tiled=True
    )
    sends = head_grads(query_in[0], grad_out[0], out_weight, members)
    parts = [sends[0]] + [swap(sends[mask], "seq", mask) for mask in range(1, members)]
    grads, near_part = after(grad_out[0], parts[1])
    queries, head_grad = join_queries(parts[:1] + [near_part] + parts[2:])
    half_grads = [grads] + [swap(grads, "seq", mask) for mask in range(1, members)]

    near, top, total = forward(bias, pairs, queries, scale)
    returns, *sends = backward(bias, top, total, pairs, queries, head_grad, near, scale)
    near, returns = after(near, returns)
    returned = lax.all_to_all(returns, "seq", split_axis=0, concat_axis=0, tiled=True)
    parts = [sends[0]] + [swap(sends[mask], "seq", mask) for mask in range(1, members)]

    own, send = weight_parts(near, half_grads, rep_count)
    bit = 1
    while 2 * bit < rep_count:
        own, send = weight_fold(own, swap(send, "rep", bit))
        bit *= 2
    own, send = weight_split(own, swap(send, "rep", bit))
    other = swap(send, "seq", members)
    mixed_out, token = project(parts, out_weight)
    weight_quarter = weight_sum(token, own, other, 1.0 / math.sqrt(rep_count * tokens))
    query_grad, key_grad, value_grad, token = unpack(
        returned, parts, tokens_here, query_in.shape[2]
    )
    weight_grad = weight_join(gather_rep(weight_quarter))
    return (mixed_out[None], query_grad[None], key_grad[None], value_grad[None], weight_grad)


def local(query_in, key_in, value_in, out_weight, grad_out, pattern):
    seq_count, rep_count = lax.axis_size("seq"), lax.axis_size("rep")
    one_head_each = seq_count * HD == query_in.shape[2] and query_in.shape[0] == 1
    paired = seq_count & (seq_count - 1) == 0 and rep_count == 4
    if one_head_each and paired and seq_count > 2:
        return dense_local(query_in, key_in, value_in, out_weight, grad_out, pattern)
    return general_local(query_in, key_in, value_in, out_weight, grad_out, pattern)


def general_local(query_in, key_in, value_in, out_weight, grad_out, pattern):
    seq_count = lax.axis_size("seq")
    rep_count = lax.axis_size("rep")
    tokens_here = query_in.shape[1]
    width = query_in.shape[2]
    head_size = HD
    head_count = width // head_size
    groups = max(seq_count // head_count, 1)
    per_device = max(head_count // seq_count, 1)
    head_groups = head_count // per_device
    local_blocks = tokens_here // BLK
    group_rows = BLK // groups
    all_blocks = seq_count * local_blocks
    columns = per_device * head_size
    span = pattern.shape[1]
    block_run = math.gcd(all_blocks, 32)
    run_count = all_blocks // block_run
    scale = 1.0 / math.sqrt(head_size)

    def to_heads(source):
        shaped = source.reshape(local_blocks, groups, group_rows, head_groups, columns)
        return shaped.transpose(3, 1, 0, 2, 4).reshape(
            seq_count, local_blocks * group_rows, columns
        )

    def to_tokens(source):
        shaped = source.reshape(head_groups, groups, local_blocks, group_rows, columns)
        return shaped.transpose(2, 1, 3, 0, 4).reshape(tokens_here, width)

    query_local = query_in[0]
    key_local = key_in[0]
    value_local = value_in[0]
    grad_local = grad_out[0]

    def spread(source):
        grouped = source.reshape(tokens_here, head_groups, columns).transpose(1, 0, 2)
        copies = jnp.broadcast_to(grouped[:, None], (head_groups, groups, tokens_here, columns))
        return copies.reshape(seq_count, tokens_here, columns)

    query_heads, key_all, value_all = (
        lax.all_to_all(to_heads(query_local), "seq", split_axis=0, concat_axis=0, tiled=True),
        lax.all_to_all(spread(key_local), "seq", split_axis=0, concat_axis=0, tiled=True),
        lax.all_to_all(spread(value_local), "seq", split_axis=0, concat_axis=0, tiled=True),
    )
    attended_grad = lax.dot_general(
        grad_local, out_weight, (((1,), (1,)), ((), ())), preferred_element_type=jnp.float32
    ).astype(jnp.bfloat16)
    grad_heads = lax.all_to_all(
        to_heads(attended_grad), "seq", split_axis=0, concat_axis=0, tiled=True
    )
    key_blocks = key_all.reshape(all_blocks, BLK, per_device, head_size)
    value_blocks = value_all.reshape(all_blocks, BLK, per_device, head_size)
    query_runs = query_heads.reshape(run_count, block_run, group_rows, per_device, head_size)
    grad_runs = grad_heads.reshape(run_count, block_run, group_rows, per_device, head_size)
    pattern_runs = pattern.reshape(run_count, block_run, span)

    def attend_step(carry, items):
        key_acc, value_acc = carry
        query_run, grad_run, pattern_run = items
        key_gathered = key_blocks[pattern_run].reshape(block_run, span * BLK, per_device, head_size)
        value_gathered = value_blocks[pattern_run].reshape(
            block_run, span * BLK, per_device, head_size
        )
        scores = (
            jnp.einsum(
                "crhd,ckhd->chrk", query_run, key_gathered, preferred_element_type=jnp.float32
            )
            * scale
        )
        shifted = scores - jnp.max(scores, axis=-1, keepdims=True)
        weights = jnp.exp(shifted)
        probs = weights / jnp.sum(weights, axis=-1, keepdims=True)
        probs_low = probs.astype(jnp.bfloat16)
        result = jnp.einsum(
            "chrk,ckhd->crhd", probs_low, value_gathered, preferred_element_type=jnp.float32
        ).astype(jnp.bfloat16)
        prob_grad = jnp.einsum(
            "crhd,ckhd->chrk", grad_run, value_gathered, preferred_element_type=jnp.float32
        )
        delta = jnp.sum(probs * prob_grad, axis=-1, keepdims=True)
        score_grad = (probs * (prob_grad - delta)).astype(jnp.bfloat16)
        query_part = (
            jnp.einsum(
                "chrk,ckhd->crhd", score_grad, key_gathered, preferred_element_type=jnp.float32
            )
            * scale
        ).astype(jnp.bfloat16)
        key_contrib = (
            jnp.einsum("chrk,crhd->ckhd", score_grad, query_run, preferred_element_type=jnp.float32)
            * scale
        )
        value_contrib = jnp.einsum(
            "chrk,crhd->ckhd", probs_low, grad_run, preferred_element_type=jnp.float32
        )
        key_acc = key_acc.at[pattern_run].add(
            key_contrib.reshape(block_run, span, BLK, per_device, head_size)
        )
        value_acc = value_acc.at[pattern_run].add(
            value_contrib.reshape(block_run, span, BLK, per_device, head_size)
        )
        return ((key_acc, value_acc), (result, query_part))

    zero_grads = jnp.zeros((all_blocks, BLK, per_device, head_size), jnp.float32)
    (key_acc, value_acc), (out_heads, query_parts) = lax.scan(
        attend_step, (zero_grads, zero_grads), (query_runs, grad_runs, pattern_runs)
    )
    out_send = out_heads.reshape(seq_count, local_blocks * group_rows, columns)
    attended = to_tokens(lax.all_to_all(out_send, "seq", split_axis=0, concat_axis=0, tiled=True))
    mixed_out = jnp.dot(attended, out_weight, preferred_element_type=jnp.float32).astype(
        jnp.bfloat16
    )
    norm_factor = 1.0 / math.sqrt(rep_count * seq_count * tokens_here)
    weight_shard = lax.psum_scatter(
        lax.dot_general(
            attended, grad_local, (((0,), (0,)), ((), ())), preferred_element_type=jnp.float32
        ),
        ("seq", "rep"),
        scatter_dimension=0,
        tiled=True,
    )
    weight_grad = lax.all_gather(
        (weight_shard * norm_factor).astype(jnp.bfloat16), "rep", axis=0, tiled=True
    ).astype(jnp.float32)
    query_send = query_parts.reshape(seq_count, local_blocks * group_rows, columns)
    key_send = key_acc.astype(jnp.bfloat16).reshape(seq_count, tokens_here, columns)
    value_send = value_acc.astype(jnp.bfloat16).reshape(seq_count, tokens_here, columns)
    query_back, key_back, value_back = (
        lax.all_to_all(query_send, "seq", split_axis=0, concat_axis=0, tiled=True),
        lax.all_to_all(key_send, "seq", split_axis=0, concat_axis=0, tiled=True),
        lax.all_to_all(value_send, "seq", split_axis=0, concat_axis=0, tiled=True),
    )

    def fold_groups(source):
        summed = jnp.sum(
            source.reshape(head_groups, groups, tokens_here, columns).astype(jnp.float32), axis=1
        )
        return summed.astype(jnp.bfloat16).transpose(1, 0, 2).reshape(tokens_here, width)

    query_grad = to_tokens(query_back)
    key_grad = fold_groups(key_back)
    value_grad = fold_groups(value_back)
    return (mixed_out[None], query_grad[None], key_grad[None], value_grad[None], weight_grad)


def solution(mesh):
    placed = (
        P("rep", "seq", None),
        P("rep", "seq", None),
        P("rep", "seq", None),
        P(),
        P("rep", "seq", None),
        P(),
    )
    return jax.shard_map(
        local,
        mesh=mesh,
        in_specs=placed,
        out_specs=(
            P("rep", "seq", None),
            P("rep", "seq", None),
            P("rep", "seq", None),
            P("rep", "seq", None),
            P("seq", None),
        ),
        check_vma=False,
    )
```

```python
import functools
import math

import jax
import jax.numpy as jnp
from jax import lax
from jax.experimental import pallas as pl
from jax.experimental.pallas import tpu as pltpu
from jax.sharding import PartitionSpec as P

HD = 128
BLK = 64
MASKED = -1e30
VMEM = pltpu.VMEM
ANY_SPEC = pl.BlockSpec(memory_space=pl.ANY)
VMEM_SPEC = pl.BlockSpec()
NT = (((1,), (1,)), ((), ()))
NN = (((1,), (0,)), ((), ()))
TN = (((0,), (0,)), ((), ()))
WIDE = 58
HEAD_MIB = 58
PROJECT_FLOPS = 1
JOIN_FLOPS = 2 << 30
SCALE_FLOPS = 8 << 30
HEADS_FLOPS = 1


def dot(left, right, dims):
    return lax.dot_general(left, right, dims, preferred_element_type=jnp.float32)


def params(mib):
    return pltpu.CompilerParams(vmem_limit_bytes=mib * 1024 * 1024)


def cost(flops=1, moved=1):
    return pl.CostEstimate(flops=flops, bytes_accessed=moved, transcendentals=0)


def struct(*shape, dtype=jnp.bfloat16):
    return jax.ShapeDtypeStruct(shape, dtype)


def in_hbm(array):
    return pltpu.with_memory_space_constraint(array, pltpu.HBM)


def span(index, size):
    return pl.ds(pl.multiple_of(index * size, size), size)


def swap(array, axis, mask):
    return lax.ppermute(array, axis, [(i, i ^ mask) for i in range(lax.axis_size(axis))])


def after(*arrays):
    return lax.optimization_barrier(arrays)


def anchored(kernel):
    return lambda anchor, *refs: kernel(*refs)


def members_of(peers):
    return peers // 2


def member(mask=0):
    return (lax.axis_index("seq") ^ mask) & (members_of(lax.axis_size("seq")) - 1)


def half_of():
    return lax.axis_index("seq") // members_of(lax.axis_size("seq"))


def pack_kernel(key_ref, value_ref, send, *refs):
    held, sem = refs[:2], refs[2]
    rows, width = key_ref.shape
    peers = send.shape[0]
    loads = [
        pltpu.make_async_copy(source, target, sem.at[index])
        for index, (source, target) in enumerate(zip((key_ref, value_ref), held))
    ]
    for load in loads:
        load.start()
    for index, source in enumerate(held):
        loads[index].wait()
        for peer in range(peers):
            for slot in range(2):
                head = peer % members_of(peers) + slot * members_of(peers)
                place = pl.ds((2 * index + slot) * rows, rows)
                send[peer, place] = source[:, head * HD : (head + 1) * HD]


def pack(keys, values, peers):
    rows, width = keys.shape
    return pl.pallas_call(
        pack_kernel,
        out_shape=struct(peers, 4 * rows, HD),
        in_specs=[ANY_SPEC] * 2,
        out_specs=VMEM_SPEC,
        scratch_shapes=[VMEM((rows, width), jnp.bfloat16)] * 2 + [pltpu.SemaphoreType.DMA((2,))],
        compiler_params=params(WIDE),
        cost_estimate=cost(),
        name="pack_keys",
    )(keys, values)


def head_grad_kernel(query_ref, grad_ref, weight_ref, *refs):
    sends, (mine, theirs), refs = refs[:-7], refs[-7:-5], refs[-5:]
    query, grad, weight, head_grad, sem = refs
    rows = query_ref.shape[0]
    members = len(sends)
    loads = [
        pltpu.make_async_copy(source, target, sem.at[index])
        for index, (source, target) in enumerate(
            zip((query_ref, grad_ref, weight_ref), (query, grad, weight))
        )
    ]
    for load in loads:
        load.start()
    loads[0].wait()
    for mask, send in enumerate(sends):
        for slot in range(2):
            send[slot * rows : (slot + 1) * rows] = query[:, span(member(mask) + slot * members, HD)]
    loads[1].wait()
    side = lax.axis_index("seq") & 1
    mine[...] = grad[:, span(side, mine.shape[1])]
    theirs[...] = grad[:, span(1 - side, theirs.shape[1])]
    loads[2].wait()
    head_grad[...] = dot(weight[...], grad[...], NT).astype(jnp.bfloat16)
    for mask, send in enumerate(sends):
        for slot in range(2):
            place = pl.ds(2 * rows + slot * HD, HD)
            send[place] = head_grad[span(member(mask) + slot * members, HD)]


def head_grads(queries, grads, out_weight, members):
    rows, width = queries.shape
    return pl.pallas_call(
        head_grad_kernel,
        out_shape=[pltpu.HBM((2 * rows + 2 * HD, HD), jnp.bfloat16)] * members
        + [pltpu.HBM((rows, grads.shape[1] // 2), jnp.bfloat16)] * 2,
        in_specs=[ANY_SPEC] * 3,
        out_specs=[VMEM_SPEC] * (members + 2),
        scratch_shapes=[
            VMEM(queries.shape, jnp.bfloat16),
            VMEM(grads.shape, jnp.bfloat16),
            VMEM(out_weight.shape, jnp.bfloat16),
            VMEM((width, rows), jnp.bfloat16),
            pltpu.SemaphoreType.DMA((3,)),
        ],
        compiler_params=params(HEAD_MIB),
        cost_estimate=cost(),
        name="head_grads",
    )(queries, grads, out_weight)


def join_queries_kernel(*refs):
    parts, (queries, grads) = refs[:-2], refs[-2:]
    rows = parts[0].shape[0] // 4
    for mask, part in enumerate(parts):
        for slot in range(2):
            queries[slot, span(member(mask), rows)] = part[slot * rows : (slot + 1) * rows]
            grad = part[2 * rows + slot * HD : 2 * rows + (slot + 1) * HD]
            grads[slot, :, span(member(mask), rows)] = grad


def join_queries(parts):
    tokens = len(parts) * parts[0].shape[0] // 4
    return pl.pallas_call(
        join_queries_kernel,
        out_shape=[struct(2, tokens, HD), struct(2, HD, tokens)],
        in_specs=[VMEM_SPEC] * len(parts),
        out_specs=[VMEM_SPEC] * 2,
        compiler_params=params(8),
        cost_estimate=cost(JOIN_FLOPS),
        name="join_queries",
    )(*map(in_hbm, parts))


def load_heads(pairs, keys, values):
    rows = pairs.shape[1] // 4
    for peer in range(pairs.shape[0]):
        for slot in range(2):
            place = slice(peer * rows, (peer + 1) * rows)
            keys[slot, place] = pairs[peer, slot * rows : (slot + 1) * rows]
            values[slot, place] = pairs[peer, (2 + slot) * rows : (3 + slot) * rows]


def scores_of(keys, queries, bias, scale):
    blocks = bias.shape[0]
    scores = dot(keys, queries, NT) * scale
    shaped = scores.reshape(blocks, BLK, queries.shape[0]) + bias[:, None, :]
    return shaped.reshape(scores.shape)


def forward_kernel(chunk, scale, bias_ref, pairs, queries, near, top_ref, sum_ref, keys, values):
    load_heads(pairs, keys, values)
    tokens = queries.shape[1]
    for slot in range(2):
        value_cols = values[slot].T
        for step in range(tokens // chunk):
            rows = slice(step * chunk, (step + 1) * chunk)
            bias = bias_ref[:, span(half_of() * (tokens // chunk) + step, chunk)]
            scores = scores_of(keys[slot], queries[slot, rows], bias, scale)
            top = jnp.max(scores, axis=0, keepdims=True)
            weights = jnp.exp(scores - top)
            total = 1.0 / jnp.sum(weights, axis=0, keepdims=True)
            probs_low = (weights * total).astype(jnp.bfloat16)
            place = pl.ds(slot * tokens + step * chunk, chunk)
            near[place] = dot(value_cols, probs_low, NN).T.astype(jnp.bfloat16)
            top_ref[slot : slot + 1, rows] = top
            sum_ref[slot : slot + 1, rows] = total


def forward(bias, pairs, queries, scale):
    tokens = bias.shape[1]
    chunk = 2 * tokens // pairs.shape[0]
    stats = struct(2, tokens // 2, dtype=jnp.float32)
    return pl.pallas_call(
        functools.partial(forward_kernel, chunk, scale),
        out_shape=[struct(tokens, HD), stats, stats],
        in_specs=[VMEM_SPEC] * 3,
        out_specs=[VMEM_SPEC] * 3,
        scratch_shapes=[VMEM((2, tokens, HD), jnp.bfloat16)] * 2,
        compiler_params=params(24),
        cost_estimate=cost(),
        name="attend",
    )(bias, pairs, queries)


def backward_kernel(chunk, scale, bias_ref, top_ref, sum_ref, pairs, queries, grads, near, *refs):
    returns, outs, (keys, values, query_grad, key_sum, value_sum) = refs[0], refs[1:-5], refs[-5:]
    load_heads(pairs, keys, values)
    tokens = queries.shape[1]
    peers = returns.shape[0]
    here = returns.shape[1] // 4
    for slot in range(2):
        key_cols = keys[slot].T
        for step in range(tokens // chunk):
            rows = slice(step * chunk, (step + 1) * chunk)
            bias = bias_ref[:, span(half_of() * (tokens // chunk) + step, chunk)]
            scores = scores_of(keys[slot], queries[slot, rows], bias, scale)
            probs = jnp.exp(scores - top_ref[slot : slot + 1, rows]) * sum_ref[slot : slot + 1, rows]
            prob_grad = dot(values[slot], grads[slot, :, rows], NN)
            delta = jnp.sum(probs * prob_grad, axis=0, keepdims=True)
            score_grad = (probs * (prob_grad - delta)).astype(jnp.bfloat16)
            value_part = dot(probs.astype(jnp.bfloat16), grads[slot, :, rows], NT)
            key_part = dot(score_grad, queries[slot, rows], NN)
            if step == 0:
                value_sum[...] = value_part
                key_sum[...] = key_part
            else:
                value_sum[...] += value_part
                key_sum[...] += key_part
            query_part = dot(key_cols, score_grad, NN) * scale
            query_grad[slot, rows] = query_part.T.astype(jnp.bfloat16)
        for peer in range(peers):
            place = slice(peer * here, (peer + 1) * here)
            key_low = (key_sum[place] * scale).astype(jnp.bfloat16)
            returns[peer, slot * here : (slot + 1) * here] = key_low
            value_low = value_sum[place].astype(jnp.bfloat16)
            returns[peer, (2 + slot) * here : (3 + slot) * here] = value_low
        for mask, out in enumerate(outs):
            theirs = span(member(mask), here)
            out[slot * here : (slot + 1) * here] = query_grad[slot, theirs]
            theirs = span(slot * len(outs) + member(mask), here)
            out[(2 + slot) * here : (3 + slot) * here] = near[theirs]


def backward(bias, top, total, pairs, queries, grads, near, scale):
    peers, tokens = pairs.shape[0], bias.shape[1]
    members = members_of(peers)
    here = tokens // peers
    return pl.pallas_call(
        functools.partial(backward_kernel, 2 * here, scale),
        out_shape=[struct(peers, 4 * here, HD)] + [pltpu.HBM((4 * here, HD), jnp.bfloat16)] * members,
        in_specs=[VMEM_SPEC] * 7,
        out_specs=[VMEM_SPEC] * (1 + members),
        scratch_shapes=[VMEM((2, tokens, HD), jnp.bfloat16)] * 2
        + [VMEM((2, tokens // 2, HD), jnp.bfloat16)]
        + [VMEM((tokens, HD), jnp.float32)] * 2,
        compiler_params=params(24),
        cost_estimate=cost(),
        name="attend_back",
    )(bias, top, total, pairs, queries, grads, near)


def unpack_kernel(returned, *refs):
    queries, (query_grad, key_grad, value_grad, token) = refs[:-4], refs[-4:]
    token[...] = jnp.zeros_like(token)
    members = len(queries)
    here = query_grad.shape[0]
    for index in range(members):
        for slot in range(2):
            columns = pl.ds((index + slot * members) * HD, HD)
            for target, first in ((key_grad, slot), (value_grad, 2 + slot)):
                rows = slice(first * here, (first + 1) * here)
                both = returned[index, rows].astype(jnp.float32) + returned[
                    index + members, rows
                ].astype(jnp.float32)
                target[:, columns] = both.astype(jnp.bfloat16)
            part = queries[index][slot * here : (slot + 1) * here]
            query_grad[:, span(member(index) + slot * members, HD)] = part


def unpack(returned, queries, rows, width):
    return pl.pallas_call(
        unpack_kernel,
        out_shape=[struct(rows, width)] * 3 + [struct(16, HD)],
        in_specs=[VMEM_SPEC] * (1 + len(queries)),
        out_specs=[VMEM_SPEC] * 4,
        compiler_params=params(16),
        cost_estimate=cost(1, 24 * rows * width),
        name="unpack_grads",
    )(returned, *map(in_hbm, queries))


def join_heads_kernel(*refs):
    parts, attended = refs[:-1], refs[-1]
    rows = attended.shape[0]
    for mask, part in enumerate(parts):
        for slot in range(2):
            columns = span(member(mask) + slot * len(parts), HD)
            attended[:, columns] = part[(2 + slot) * rows : (3 + slot) * rows]


def join_heads(parts):
    rows = parts[0].shape[0] // 4
    return pl.pallas_call(
        join_heads_kernel,
        out_shape=struct(rows, 2 * HD * len(parts)),
        in_specs=[VMEM_SPEC] * len(parts),
        out_specs=VMEM_SPEC,
        compiler_params=params(8),
        cost_estimate=cost(HEADS_FLOPS),
        name="join_heads",
    )(*map(in_hbm, parts))


def project_kernel(attended, weight_ref, out_ref, token):
    token[...] = jnp.zeros_like(token)
    out_ref[...] = dot(attended[...], weight_ref[...], NN).astype(jnp.bfloat16)


def project(attended, out_weight):
    rows = attended.shape[0]
    depth, width = out_weight.shape
    tile = width // 4
    return pl.pallas_call(
        project_kernel,
        out_shape=[struct(rows, width), struct(16, HD)],
        grid=(width // tile,),
        in_specs=[
            pl.BlockSpec((rows, depth), lambda i: (0, 0)),
            pl.BlockSpec((depth, tile), lambda i: (0, i)),
        ],
        out_specs=[
            pl.BlockSpec((rows, tile), lambda i: (0, i)),
            pl.BlockSpec((16, HD), lambda i: (0, 0)),
        ],
        compiler_params=params(24),
        cost_estimate=cost(PROJECT_FLOPS, 1),
        name="project",
    )(attended, out_weight)


def weight_part_kernel(docs, near, near_pair, *refs):
    grads, (own, send) = refs[:-2], refs[-2:]
    members = len(grads)
    rows = grads[0].shape[0]
    width = grads[0].shape[1] // docs
    lefts = []
    for source in (near, near_pair):
        for slot in range(2):
            places = [span(slot * members + member(mask), rows) for mask in range(members)]
            lefts.append(jnp.concatenate([source[place] for place in places], axis=0))
    left = jnp.concatenate(lefts, axis=1).T
    for mask in range(docs):
        columns = span(lax.axis_index("rep") ^ mask, width)
        right = jnp.concatenate([grad[:, columns] for grad in grads], axis=0)
        place = pl.ds(mask // 2 * left.shape[0], left.shape[0])
        if mask % 2:
            send[place] = dot(left, right, NN).astype(jnp.bfloat16)
        else:
            own[place] = dot(left, right, NN)


def weight_parts(near, near_pair, grads, docs):
    width = grads[0].shape[1] // docs
    rows = docs // 2 * 4 * HD
    return pl.pallas_call(
        functools.partial(weight_part_kernel, docs),
        out_shape=[struct(rows, width, dtype=jnp.float32), struct(rows, width)],
        in_specs=[VMEM_SPEC] * (2 + len(grads)),
        out_specs=[VMEM_SPEC] * 2,
        compiler_params=params(24),
        cost_estimate=cost(),
        name="weight_part",
    )(near, near_pair, *map(in_hbm, grads))


def weight_fold_kernel(own, other, keep, send):
    rows = keep.shape[0]
    keep[...] = own[:rows] + other[:rows].astype(jnp.float32)
    send[...] = (own[rows:] + other[rows:].astype(jnp.float32)).astype(jnp.bfloat16)


def weight_fold(own, other):
    rows, width = own.shape
    return pl.pallas_call(
        weight_fold_kernel,
        out_shape=[struct(rows // 2, width, dtype=jnp.float32), struct(rows // 2, width)],
        in_specs=[VMEM_SPEC] * 2,
        out_specs=[VMEM_SPEC] * 2,
        compiler_params=params(8),
        cost_estimate=cost(),
        name="weight_fold",
    )(own, other)


def weight_spread_kernel(own, other, *targets):
    rows = targets[0].shape[0]
    half = half_of()
    for index, target in enumerate(targets):
        block = span(index // 2 * 2 + (1 - half if index % 2 else half), rows)
        target[...] = (own[block] + other[block].astype(jnp.float32)).astype(target.dtype)


def weight_spread(own, other):
    rows, width = own.shape
    return pl.pallas_call(
        weight_spread_kernel,
        out_shape=[struct(rows // 4, width, dtype=jnp.float32)] + [struct(rows // 4, width)] * 3,
        in_specs=[VMEM_SPEC] * 2,
        out_specs=[VMEM_SPEC] * 4,
        compiler_params=params(8),
        cost_estimate=cost(),
        name="weight_spread",
    )(own, other)


def weight_scale_kernel(factor, own, across, pair, diagonal, total):
    rows = own.shape[0]
    total[:rows] = ((own[...] + across[...].astype(jnp.float32)) * factor).astype(jnp.bfloat16)
    other = pair[...].astype(jnp.float32) + diagonal[...].astype(jnp.float32)
    total[rows:] = (other * factor).astype(jnp.bfloat16)


def weight_scale(anchor, own, across, pair, diagonal, factor):
    rows, width = own.shape
    return pl.pallas_call(
        anchored(functools.partial(weight_scale_kernel, factor)),
        out_shape=struct(2 * rows, width),
        in_specs=[ANY_SPEC] + [VMEM_SPEC] * 4,
        out_specs=VMEM_SPEC,
        compiler_params=params(8),
        cost_estimate=cost(SCALE_FLOPS),
        name="weight_scale",
    )(anchor, own, across, pair, diagonal)


def weight_join_kernel(*refs):
    parts, total = refs[:-1], refs[-1]
    rows, width = total.shape[0], parts[0].shape[1]
    side = lax.axis_index("seq") & 1
    for mask, part in enumerate(parts):
        share = lax.axis_index("rep") ^ mask
        for index, place in ((0, side), (1, 1 - side)):
            block = part[index * rows : (index + 1) * rows]
            total[:, span(place * len(parts) + share, width)] = block.astype(jnp.float32)


def weight_join(anchor, pairs):
    rows, width = HD, pairs[0].shape[1]
    return pl.pallas_call(
        anchored(weight_join_kernel),
        out_shape=struct(rows, 2 * width * len(pairs), dtype=jnp.float32),
        in_specs=[ANY_SPEC] + [VMEM_SPEC] * len(pairs),
        out_specs=VMEM_SPEC,
        compiler_params=params(8),
        cost_estimate=cost(),
        name="weight_join",
    )(anchor, *pairs)


def dense_bias(pattern, tokens):
    blocks = pattern.shape[0]
    named = pattern[:, :, None] == jnp.arange(blocks, dtype=pattern.dtype)
    counts = jnp.sum(named.astype(jnp.float32), axis=1).T
    bias = jnp.where(counts > 0, jnp.log(jnp.maximum(counts, 1.0)), MASKED)
    return jnp.repeat(bias, tokens // blocks, axis=1)


def dense_local(query_in, key_in, value_in, out_weight, grad_out, pattern):
    seq_count, rep_count = lax.axis_size("seq"), lax.axis_size("rep")
    tokens_here = query_in.shape[1]
    tokens = tokens_here * seq_count
    members = members_of(seq_count)
    scale = 1.0 / math.sqrt(HD)
    bias = dense_bias(pattern, tokens)

    pairs = lax.all_to_all(
        pack(key_in[0], value_in[0], seq_count), "seq", split_axis=0, concat_axis=0, tiled=True
    )
    *sends, grad_mine, grad_theirs = head_grads(query_in[0], grad_out[0], out_weight, members)
    parts = [sends[0]] + [swap(sends[mask], "seq", mask) for mask in range(1, members)]
    grad_mine, grad_theirs, *parts[1:3] = after(grad_mine, grad_theirs, *parts[1:3])
    queries, head_grad = join_queries(parts)
    half_grads = [grad_mine] + [
        swap(grad_theirs if mask & 1 else grad_mine, "seq", mask) for mask in range(1, members)
    ]

    near, top, total = forward(bias, pairs, queries, scale)
    near_pair = swap(near, "seq", 1)
    returns, *sends = backward(bias, top, total, pairs, queries, head_grad, near, scale)
    near, returns = after(near, returns)
    returned = lax.all_to_all(returns, "seq", split_axis=0, concat_axis=0, tiled=True)
    parts = [sends[0]] + [swap(sends[mask], "seq", mask) for mask in range(1, members)]

    own, send = weight_parts(near, near_pair, half_grads, rep_count)
    bit = 1
    while 2 * bit < rep_count:
        own, send = weight_fold(own, swap(send, "rep", bit))
        bit *= 2
    own, *sends = weight_spread(own, swap(send, "rep", bit))
    arrived = [swap(block, "seq", mask) for block, mask in zip(sends, (members, 1, members + 1))]
    mixed_out, token = project(join_heads(parts), out_weight)
    factor = 1.0 / math.sqrt(rep_count * tokens)
    pair = weight_scale(token, own, *arrived, factor)
    query_grad, key_grad, value_grad, token = unpack(
        returned, parts, tokens_here, query_in.shape[2]
    )
    across, token = after(swap(pair, "rep", 2), token)
    quarters = [pair, swap(pair, "rep", 1), across, swap(across, "rep", 1)]
    weight_grad = weight_join(token, quarters)
    return (mixed_out[None], query_grad[None], key_grad[None], value_grad[None], weight_grad)


    return (mixed_out[None], query_grad[None], key_grad[None], value_grad[None], weight_grad)


    return (mixed_out[None], query_grad[None], key_grad[None], value_grad[None], weight_grad)


def local(query_in, key_in, value_in, out_weight, grad_out, pattern):
    seq_count, rep_count = lax.axis_size("seq"), lax.axis_size("rep")
    one_head_each = seq_count * HD == query_in.shape[2] and query_in.shape[0] == 1
    paired = seq_count & (seq_count - 1) == 0 and rep_count == 4
    if one_head_each and paired and seq_count > 2:
        return dense_local(query_in, key_in, value_in, out_weight, grad_out, pattern)
    return general_local(query_in, key_in, value_in, out_weight, grad_out, pattern)


def general_local(query_in, key_in, value_in, out_weight, grad_out, pattern):
    seq_count = lax.axis_size("seq")
    rep_count = lax.axis_size("rep")
    tokens_here = query_in.shape[1]
    width = query_in.shape[2]
    head_size = HD
    head_count = width // head_size
    groups = max(seq_count // head_count, 1)
    per_device = max(head_count // seq_count, 1)
    head_groups = head_count // per_device
    local_blocks = tokens_here // BLK
    group_rows = BLK // groups
    all_blocks = seq_count * local_blocks
    columns = per_device * head_size
    span = pattern.shape[1]
    block_run = math.gcd(all_blocks, 32)
    run_count = all_blocks // block_run
    scale = 1.0 / math.sqrt(head_size)

    def to_heads(source):
        shaped = source.reshape(local_blocks, groups, group_rows, head_groups, columns)
        return shaped.transpose(3, 1, 0, 2, 4).reshape(
            seq_count, local_blocks * group_rows, columns
        )

    def to_tokens(source):
        shaped = source.reshape(head_groups, groups, local_blocks, group_rows, columns)
        return shaped.transpose(2, 1, 3, 0, 4).reshape(tokens_here, width)

    query_local = query_in[0]
    key_local = key_in[0]
    value_local = value_in[0]
    grad_local = grad_out[0]

    def spread(source):
        grouped = source.reshape(tokens_here, head_groups, columns).transpose(1, 0, 2)
        copies = jnp.broadcast_to(grouped[:, None], (head_groups, groups, tokens_here, columns))
        return copies.reshape(seq_count, tokens_here, columns)

    query_heads, key_all, value_all = (
        lax.all_to_all(to_heads(query_local), "seq", split_axis=0, concat_axis=0, tiled=True),
        lax.all_to_all(spread(key_local), "seq", split_axis=0, concat_axis=0, tiled=True),
        lax.all_to_all(spread(value_local), "seq", split_axis=0, concat_axis=0, tiled=True),
    )
    attended_grad = lax.dot_general(
        grad_local, out_weight, (((1,), (1,)), ((), ())), preferred_element_type=jnp.float32
    ).astype(jnp.bfloat16)
    grad_heads = lax.all_to_all(
        to_heads(attended_grad), "seq", split_axis=0, concat_axis=0, tiled=True
    )
    key_blocks = key_all.reshape(all_blocks, BLK, per_device, head_size)
    value_blocks = value_all.reshape(all_blocks, BLK, per_device, head_size)
    query_runs = query_heads.reshape(run_count, block_run, group_rows, per_device, head_size)
    grad_runs = grad_heads.reshape(run_count, block_run, group_rows, per_device, head_size)
    pattern_runs = pattern.reshape(run_count, block_run, span)

    def attend_step(carry, items):
        key_acc, value_acc = carry
        query_run, grad_run, pattern_run = items
        key_gathered = key_blocks[pattern_run].reshape(block_run, span * BLK, per_device, head_size)
        value_gathered = value_blocks[pattern_run].reshape(
            block_run, span * BLK, per_device, head_size
        )
        scores = (
            jnp.einsum(
                "crhd,ckhd->chrk", query_run, key_gathered, preferred_element_type=jnp.float32
            )
            * scale
        )
        shifted = scores - jnp.max(scores, axis=-1, keepdims=True)
        weights = jnp.exp(shifted)
        probs = weights / jnp.sum(weights, axis=-1, keepdims=True)
        probs_low = probs.astype(jnp.bfloat16)
        result = jnp.einsum(
            "chrk,ckhd->crhd", probs_low, value_gathered, preferred_element_type=jnp.float32
        ).astype(jnp.bfloat16)
        prob_grad = jnp.einsum(
            "crhd,ckhd->chrk", grad_run, value_gathered, preferred_element_type=jnp.float32
        )
        delta = jnp.sum(probs * prob_grad, axis=-1, keepdims=True)
        score_grad = (probs * (prob_grad - delta)).astype(jnp.bfloat16)
        query_part = (
            jnp.einsum(
                "chrk,ckhd->crhd", score_grad, key_gathered, preferred_element_type=jnp.float32
            )
            * scale
        ).astype(jnp.bfloat16)
        key_contrib = (
            jnp.einsum("chrk,crhd->ckhd", score_grad, query_run, preferred_element_type=jnp.float32)
            * scale
        )
        value_contrib = jnp.einsum(
            "chrk,crhd->ckhd", probs_low, grad_run, preferred_element_type=jnp.float32
        )
        key_acc = key_acc.at[pattern_run].add(
            key_contrib.reshape(block_run, span, BLK, per_device, head_size)
        )
        value_acc = value_acc.at[pattern_run].add(
            value_contrib.reshape(block_run, span, BLK, per_device, head_size)
        )
        return ((key_acc, value_acc), (result, query_part))

    zero_grads = jnp.zeros((all_blocks, BLK, per_device, head_size), jnp.float32)
    (key_acc, value_acc), (out_heads, query_parts) = lax.scan(
        attend_step, (zero_grads, zero_grads), (query_runs, grad_runs, pattern_runs)
    )
    out_send = out_heads.reshape(seq_count, local_blocks * group_rows, columns)
    attended = to_tokens(lax.all_to_all(out_send, "seq", split_axis=0, concat_axis=0, tiled=True))
    mixed_out = jnp.dot(attended, out_weight, preferred_element_type=jnp.float32).astype(
        jnp.bfloat16
    )
    norm_factor = 1.0 / math.sqrt(rep_count * seq_count * tokens_here)
    weight_shard = lax.psum_scatter(
        lax.dot_general(
            attended, grad_local, (((0,), (0,)), ((), ())), preferred_element_type=jnp.float32
        ),
        ("seq", "rep"),
        scatter_dimension=0,
        tiled=True,
    )
    weight_grad = lax.all_gather(
        (weight_shard * norm_factor).astype(jnp.bfloat16), "rep", axis=0, tiled=True
    ).astype(jnp.float32)
    query_send = query_parts.reshape(seq_count, local_blocks * group_rows, columns)
    key_send = key_acc.astype(jnp.bfloat16).reshape(seq_count, tokens_here, columns)
    value_send = value_acc.astype(jnp.bfloat16).reshape(seq_count, tokens_here, columns)
    query_back, key_back, value_back = (
        lax.all_to_all(query_send, "seq", split_axis=0, concat_axis=0, tiled=True),
        lax.all_to_all(key_send, "seq", split_axis=0, concat_axis=0, tiled=True),
        lax.all_to_all(value_send, "seq", split_axis=0, concat_axis=0, tiled=True),
    )

    def fold_groups(source):
        summed = jnp.sum(
            source.reshape(head_groups, groups, tokens_here, columns).astype(jnp.float32), axis=1
        )
        return summed.astype(jnp.bfloat16).transpose(1, 0, 2).reshape(tokens_here, width)

    query_grad = to_tokens(query_back)
    key_grad = fold_groups(key_back)
    value_grad = fold_groups(value_back)
    return (mixed_out[None], query_grad[None], key_grad[None], value_grad[None], weight_grad)


def solution(mesh):
    placed = (
        P("rep", "seq", None),
        P("rep", "seq", None),
        P("rep", "seq", None),
        P(),
        P("rep", "seq", None),
        P(),
    )
    return jax.shard_map(
        local,
        mesh=mesh,
        in_specs=placed,
        out_specs=(
            P("rep", "seq", None),
            P("rep", "seq", None),
            P("rep", "seq", None),
            P("rep", "seq", None),
            P("seq", None),
        ),
        check_vma=False,
    )
```

```python
import functools
import math

import jax
import jax.numpy as jnp
from jax import lax
from jax.experimental import pallas as pl
from jax.experimental.pallas import tpu as pltpu
from jax.sharding import PartitionSpec as P

HD = 128
BLK = 64
MASKED = -1e30
LOG2E = math.log2(math.e)
VMEM = pltpu.VMEM
ANY_SPEC = pl.BlockSpec(memory_space=pl.ANY)
VMEM_SPEC = pl.BlockSpec()
NT = (((1,), (1,)), ((), ()))
NN = (((1,), (0,)), ((), ()))
TN = (((0,), (0,)), ((), ()))
WIDE = 58
HEAD_MIB = 58
PROJECT_FLOPS = 1
JOIN_FLOPS = 2 << 30
SCALE_FLOPS = 8 << 30
HEADS_FLOPS = 1


def dot(left, right, dims):
    return lax.dot_general(left, right, dims, preferred_element_type=jnp.float32)


def params(mib):
    return pltpu.CompilerParams(vmem_limit_bytes=mib * 1024 * 1024)


def cost(flops=1, moved=1):
    return pl.CostEstimate(flops=flops, bytes_accessed=moved, transcendentals=0)


def struct(*shape, dtype=jnp.bfloat16):
    return jax.ShapeDtypeStruct(shape, dtype)


def in_hbm(array):
    return pltpu.with_memory_space_constraint(array, pltpu.HBM)


def span(index, size):
    return pl.ds(pl.multiple_of(index * size, size), size)


def swap(array, axis, mask):
    return lax.ppermute(array, axis, [(i, i ^ mask) for i in range(lax.axis_size(axis))])


def after(*arrays):
    return lax.optimization_barrier(arrays)


def anchored(kernel):
    return lambda anchor, *refs: kernel(*refs)


def members_of(peers):
    return peers // 2


def member(mask=0):
    return (lax.axis_index("seq") ^ mask) & (members_of(lax.axis_size("seq")) - 1)


def half_of():
    return lax.axis_index("seq") // members_of(lax.axis_size("seq"))


def pack_kernel(key_ref, value_ref, send, *refs):
    held, sem = refs[:2], refs[2]
    rows, width = key_ref.shape
    peers = send.shape[0]
    loads = [
        pltpu.make_async_copy(source, target, sem.at[index])
        for index, (source, target) in enumerate(zip((key_ref, value_ref), held))
    ]
    for load in loads:
        load.start()
    for index, source in enumerate(held):
        loads[index].wait()
        for peer in range(peers):
            for slot in range(2):
                head = peer % members_of(peers) + slot * members_of(peers)
                place = pl.ds((2 * index + slot) * rows, rows)
                send[peer, place] = source[:, head * HD : (head + 1) * HD]


def pack(keys, values, peers):
    rows, width = keys.shape
    return pl.pallas_call(
        pack_kernel,
        out_shape=struct(peers, 4 * rows, HD),
        in_specs=[ANY_SPEC] * 2,
        out_specs=VMEM_SPEC,
        scratch_shapes=[VMEM((rows, width), jnp.bfloat16)] * 2 + [pltpu.SemaphoreType.DMA((2,))],
        compiler_params=params(WIDE),
        cost_estimate=cost(),
        name="pack_keys",
    )(keys, values)


def head_grad_kernel(query_ref, grad_ref, weight_ref, *refs):
    sends, (mine, theirs), refs = refs[:-7], refs[-7:-5], refs[-5:]
    query, grad, weight, head_grad, sem = refs
    rows = query_ref.shape[0]
    members = len(sends)
    loads = [
        pltpu.make_async_copy(source, target, sem.at[index])
        for index, (source, target) in enumerate(
            zip((query_ref, grad_ref, weight_ref), (query, grad, weight))
        )
    ]
    for load in loads:
        load.start()
    loads[0].wait()
    for mask, send in enumerate(sends):
        for slot in range(2):
            send[slot * rows : (slot + 1) * rows] = query[:, span(member(mask) + slot * members, HD)]
    loads[1].wait()
    side = lax.axis_index("seq") & 1
    mine[...] = grad[:, span(side, mine.shape[1])]
    theirs[...] = grad[:, span(1 - side, theirs.shape[1])]
    loads[2].wait()
    head_grad[...] = dot(weight[...], grad[...], NT).astype(jnp.bfloat16)
    for mask, send in enumerate(sends):
        for slot in range(2):
            place = pl.ds(2 * rows + slot * HD, HD)
            send[place] = head_grad[span(member(mask) + slot * members, HD)]


def head_grads(queries, grads, out_weight, members):
    rows, width = queries.shape
    return pl.pallas_call(
        head_grad_kernel,
        out_shape=[pltpu.HBM((2 * rows + 2 * HD, HD), jnp.bfloat16)] * members
        + [pltpu.HBM((rows, grads.shape[1] // 2), jnp.bfloat16)] * 2,
        in_specs=[ANY_SPEC] * 3,
        out_specs=[VMEM_SPEC] * (members + 2),
        scratch_shapes=[
            VMEM(queries.shape, jnp.bfloat16),
            VMEM(grads.shape, jnp.bfloat16),
            VMEM(out_weight.shape, jnp.bfloat16),
            VMEM((width, rows), jnp.bfloat16),
            pltpu.SemaphoreType.DMA((3,)),
        ],
        compiler_params=params(HEAD_MIB),
        cost_estimate=cost(),
        name="head_grads",
    )(queries, grads, out_weight)


def load_queries(parts, queries, grads=None):
    rows = parts[0].shape[0] // 4
    for mask, part in enumerate(parts):
        for slot in range(2):
            queries[slot, span(member(mask), rows)] = part[slot * rows : (slot + 1) * rows]
            if grads is not None:
                grad = part[2 * rows + slot * HD : 2 * rows + (slot + 1) * HD]
                grads[slot, :, span(member(mask), rows)] = grad


def load_heads(pairs, keys, values):
    rows = pairs.shape[1] // 4
    for peer in range(pairs.shape[0]):
        for slot in range(2):
            place = slice(peer * rows, (peer + 1) * rows)
            keys[slot, place] = pairs[peer, slot * rows : (slot + 1) * rows]
            values[slot, place] = pairs[peer, (2 + slot) * rows : (3 + slot) * rows]


def scores_of(keys, queries, bias, scale):
    blocks = bias.shape[0]
    scores = dot(keys, queries, NT) * (scale * LOG2E)
    shaped = scores.reshape(blocks, BLK, queries.shape[0]) + bias[:, None, :]
    return shaped.reshape(scores.shape)


def forward_kernel(members, chunk, scale, bias_ref, pairs, *refs):
    parts, (near, norm_ref, keys, values, queries) = refs[:members], refs[members:]
    load_heads(pairs, keys, values)
    load_queries(parts, queries)
    tokens = queries.shape[1]
    for slot in range(2):
        value_cols = values[slot].T
        for step in range(tokens // chunk):
            rows = slice(step * chunk, (step + 1) * chunk)
            bias = bias_ref[:, span(half_of() * (tokens // chunk) + step, chunk)]
            scores = scores_of(keys[slot], queries[slot, rows], bias, scale)
            top = jnp.max(scores, axis=0, keepdims=True)
            weights = jnp.exp2(scores - top)
            total = jnp.sum(weights, axis=0, keepdims=True)
            probs_low = (weights * (1.0 / total)).astype(jnp.bfloat16)
            place = pl.ds(slot * tokens + step * chunk, chunk)
            near[place] = dot(value_cols, probs_low, NN).T.astype(jnp.bfloat16)
            norm_ref[slot : slot + 1, rows] = top + jnp.log2(total)


def forward(bias, pairs, parts, scale):
    tokens = bias.shape[1]
    chunk = 4 * tokens // pairs.shape[0]
    stats = struct(2, tokens // 2, dtype=jnp.float32)
    return pl.pallas_call(
        functools.partial(forward_kernel, len(parts), chunk, scale),
        out_shape=[struct(tokens, HD), stats],
        in_specs=[VMEM_SPEC] * (2 + len(parts)),
        out_specs=[VMEM_SPEC] * 2,
        scratch_shapes=[VMEM((2, tokens, HD), jnp.bfloat16)] * 2
        + [VMEM((2, tokens // 2, HD), jnp.bfloat16)],
        compiler_params=params(30),
        cost_estimate=cost(),
        name="attend",
    )(bias, pairs, *parts)


def backward_kernel(members, chunk, scale, bias_ref, norm_ref, pairs, near, *refs):
    parts, returns, outs, refs = refs[:members], refs[members], refs[members + 1 : -5], refs[-5:]
    keys, values, queries, grads, query_grad = refs
    load_heads(pairs, keys, values)
    load_queries(parts, queries, grads)
    tokens = queries.shape[1]
    peers = returns.shape[0]
    here = returns.shape[1] // 4
    for slot in range(2):
        key_cols = keys[slot].T
        for step in range(tokens // chunk):
            rows = slice(step * chunk, (step + 1) * chunk)
            bias = bias_ref[:, span(half_of() * (tokens // chunk) + step, chunk)]
            bias = bias - norm_ref[slot : slot + 1, rows]
            probs = jnp.exp2(scores_of(keys[slot], queries[slot, rows], bias, scale))
            prob_grad = dot(values[slot], grads[slot, :, rows], NN)
            delta = jnp.sum(probs * prob_grad, axis=0, keepdims=True)
            score_grad = (probs * (prob_grad - delta)).astype(jnp.bfloat16)
            value_part = dot(probs.astype(jnp.bfloat16), grads[slot, :, rows], NT)
            key_part = dot(score_grad, queries[slot, rows], NN)
            key_total = key_part if step == 0 else key_total + key_part
            value_total = value_part if step == 0 else value_total + value_part
            query_part = dot(key_cols, score_grad, NN) * scale
            query_grad[slot, rows] = query_part.T.astype(jnp.bfloat16)
        for first, total in ((slot, key_total * scale), (2 + slot, value_total)):
            low = total.astype(jnp.bfloat16).reshape(peers, here, HD)
            returns[:, first * here : (first + 1) * here] = low
        for mask, out in enumerate(outs):
            theirs = span(member(mask), here)
            out[slot * here : (slot + 1) * here] = query_grad[slot, theirs]
            theirs = span(slot * len(outs) + member(mask), here)
            out[(2 + slot) * here : (3 + slot) * here] = near[theirs]


def backward(bias, norm, pairs, parts, near, scale):
    peers, tokens = pairs.shape[0], bias.shape[1]
    members = members_of(peers)
    here = tokens // peers
    return pl.pallas_call(
        functools.partial(backward_kernel, members, 4 * here, scale),
        out_shape=[struct(peers, 4 * here, HD)] + [pltpu.HBM((4 * here, HD), jnp.bfloat16)] * members,
        in_specs=[VMEM_SPEC] * (4 + members),
        out_specs=[VMEM_SPEC] * (1 + members),
        scratch_shapes=[VMEM((2, tokens, HD), jnp.bfloat16)] * 2
        + [VMEM((2, tokens // 2, HD), jnp.bfloat16), VMEM((2, HD, tokens // 2), jnp.bfloat16)]
        + [VMEM((2, tokens // 2, HD), jnp.bfloat16)],
        compiler_params=params(30),
        cost_estimate=cost(),
        name="attend_back",
    )(bias, norm, pairs, near, *parts)


def unpack_kernel(returned, *refs):
    queries, (query_grad, key_grad, value_grad, token) = refs[:-4], refs[-4:]
    token[...] = jnp.zeros_like(token)
    members = len(queries)
    here = query_grad.shape[0]
    for index in range(members):
        for slot in range(2):
            columns = pl.ds((index + slot * members) * HD, HD)
            for target, first in ((key_grad, slot), (value_grad, 2 + slot)):
                rows = slice(first * here, (first + 1) * here)
                both = returned[index, rows].astype(jnp.float32) + returned[
                    index + members, rows
                ].astype(jnp.float32)
                target[:, columns] = both.astype(jnp.bfloat16)
            part = queries[index][slot * here : (slot + 1) * here]
            query_grad[:, span(member(index) + slot * members, HD)] = part


def unpack(returned, queries, rows, width):
    return pl.pallas_call(
        unpack_kernel,
        out_shape=[struct(rows, width)] * 3 + [struct(16, HD)],
        in_specs=[VMEM_SPEC] * (1 + len(queries)),
        out_specs=[VMEM_SPEC] * 4,
        compiler_params=params(16),
        cost_estimate=cost(1, 24 * rows * width),
        name="unpack_grads",
    )(returned, *map(in_hbm, queries))


def join_heads_kernel(*refs):
    parts, attended = refs[:-1], refs[-1]
    rows = attended.shape[0]
    for mask, part in enumerate(parts):
        for slot in range(2):
            columns = span(member(mask) + slot * len(parts), HD)
            attended[:, columns] = part[(2 + slot) * rows : (3 + slot) * rows]


def join_heads(parts):
    rows = parts[0].shape[0] // 4
    return pl.pallas_call(
        join_heads_kernel,
        out_shape=struct(rows, 2 * HD * len(parts)),
        in_specs=[VMEM_SPEC] * len(parts),
        out_specs=VMEM_SPEC,
        compiler_params=params(8),
        cost_estimate=cost(HEADS_FLOPS),
        name="join_heads",
    )(*map(in_hbm, parts))


def project_kernel(attended, weight_ref, out_ref, token):
    token[...] = jnp.zeros_like(token)
    out_ref[...] = dot(attended[...], weight_ref[...], NN).astype(jnp.bfloat16)


def project(attended, out_weight):
    rows = attended.shape[0]
    depth, width = out_weight.shape
    tile = width // 4
    return pl.pallas_call(
        project_kernel,
        out_shape=[struct(rows, width), struct(16, HD)],
        grid=(width // tile,),
        in_specs=[
            pl.BlockSpec((rows, depth), lambda i: (0, 0)),
            pl.BlockSpec((depth, tile), lambda i: (0, i)),
        ],
        out_specs=[
            pl.BlockSpec((rows, tile), lambda i: (0, i)),
            pl.BlockSpec((16, HD), lambda i: (0, 0)),
        ],
        compiler_params=params(30),
        cost_estimate=cost(PROJECT_FLOPS, 1),
        name="project",
    )(attended, out_weight)


def weight_part_kernel(docs, near, near_pair, *refs):
    grads, (own, send) = refs[:-2], refs[-2:]
    members = len(grads)
    rows = grads[0].shape[0]
    width = grads[0].shape[1] // docs
    lefts = []
    for source in (near, near_pair):
        for slot in range(2):
            places = [span(slot * members + member(mask), rows) for mask in range(members)]
            lefts.append(jnp.concatenate([source[place] for place in places], axis=0))
    left = jnp.concatenate(lefts, axis=1).T
    for mask in range(docs):
        columns = span(lax.axis_index("rep") ^ mask, width)
        right = jnp.concatenate([grad[:, columns] for grad in grads], axis=0)
        place = pl.ds(mask // 2 * left.shape[0], left.shape[0])
        if mask % 2:
            send[place] = dot(left, right, NN).astype(jnp.bfloat16)
        else:
            own[place] = dot(left, right, NN)


def weight_parts(near, near_pair, grads, docs):
    width = grads[0].shape[1] // docs
    rows = docs // 2 * 4 * HD
    return pl.pallas_call(
        functools.partial(weight_part_kernel, docs),
        out_shape=[struct(rows, width, dtype=jnp.float32), struct(rows, width)],
        in_specs=[VMEM_SPEC] * (2 + len(grads)),
        out_specs=[VMEM_SPEC] * 2,
        compiler_params=params(30),
        cost_estimate=cost(),
        name="weight_part",
    )(near, near_pair, *map(in_hbm, grads))


def weight_fold_kernel(own, other, keep, send):
    rows = keep.shape[0]
    keep[...] = own[:rows] + other[:rows].astype(jnp.float32)
    send[...] = (own[rows:] + other[rows:].astype(jnp.float32)).astype(jnp.bfloat16)


def weight_fold(own, other):
    rows, width = own.shape
    return pl.pallas_call(
        weight_fold_kernel,
        out_shape=[struct(rows // 2, width, dtype=jnp.float32), struct(rows // 2, width)],
        in_specs=[VMEM_SPEC] * 2,
        out_specs=[VMEM_SPEC] * 2,
        compiler_params=params(8),
        cost_estimate=cost(),
        name="weight_fold",
    )(own, other)


def weight_spread_kernel(own, other, *targets):
    rows = targets[0].shape[0]
    half = half_of()
    for index, target in enumerate(targets):
        block = span(index // 2 * 2 + (1 - half if index % 2 else half), rows)
        target[...] = (own[block] + other[block].astype(jnp.float32)).astype(target.dtype)


def weight_spread(own, other):
    rows, width = own.shape
    return pl.pallas_call(
        weight_spread_kernel,
        out_shape=[struct(rows // 4, width, dtype=jnp.float32)] + [struct(rows // 4, width)] * 3,
        in_specs=[VMEM_SPEC] * 2,
        out_specs=[VMEM_SPEC] * 4,
        compiler_params=params(8),
        cost_estimate=cost(),
        name="weight_spread",
    )(own, other)


def weight_scale_kernel(factor, own, across, pair, diagonal, total):
    rows = own.shape[0]
    total[:rows] = ((own[...] + across[...].astype(jnp.float32)) * factor).astype(jnp.bfloat16)
    other = pair[...].astype(jnp.float32) + diagonal[...].astype(jnp.float32)
    total[rows:] = (other * factor).astype(jnp.bfloat16)


def weight_scale(anchor, own, across, pair, diagonal, factor):
    rows, width = own.shape
    return pl.pallas_call(
        anchored(functools.partial(weight_scale_kernel, factor)),
        out_shape=struct(2 * rows, width),
        in_specs=[ANY_SPEC] + [VMEM_SPEC] * 4,
        out_specs=VMEM_SPEC,
        compiler_params=params(8),
        cost_estimate=cost(SCALE_FLOPS),
        name="weight_scale",
    )(anchor, own, across, pair, diagonal)


def weight_join_kernel(*refs):
    parts, total = refs[:-1], refs[-1]
    rows, width = total.shape[0], parts[0].shape[1]
    side = lax.axis_index("seq") & 1
    for mask, part in enumerate(parts):
        share = lax.axis_index("rep") ^ mask
        for index, place in ((0, side), (1, 1 - side)):
            block = part[index * rows : (index + 1) * rows]
            total[:, span(place * len(parts) + share, width)] = block.astype(jnp.float32)


def weight_join(anchor, pairs):
    rows, width = HD, pairs[0].shape[1]
    return pl.pallas_call(
        anchored(weight_join_kernel),
        out_shape=struct(rows, 2 * width * len(pairs), dtype=jnp.float32),
        in_specs=[ANY_SPEC] + [VMEM_SPEC] * len(pairs),
        out_specs=VMEM_SPEC,
        compiler_params=params(8),
        cost_estimate=cost(),
        name="weight_join",
    )(anchor, *pairs)


def dense_bias(pattern, tokens):
    blocks = pattern.shape[0]
    named = pattern[:, :, None] == jnp.arange(blocks, dtype=pattern.dtype)
    counts = jnp.sum(named.astype(jnp.float32), axis=1).T
    bias = jnp.where(counts > 0, jnp.log2(jnp.maximum(counts, 1.0)), MASKED)
    return jnp.repeat(bias, tokens // blocks, axis=1)


def dense_local(query_in, key_in, value_in, out_weight, grad_out, pattern):
    seq_count, rep_count = lax.axis_size("seq"), lax.axis_size("rep")
    tokens_here = query_in.shape[1]
    tokens = tokens_here * seq_count
    members = members_of(seq_count)
    scale = 1.0 / math.sqrt(HD)
    bias = dense_bias(pattern, tokens)

    pairs = lax.all_to_all(
        pack(key_in[0], value_in[0], seq_count), "seq", split_axis=0, concat_axis=0, tiled=True
    )
    *sends, grad_mine, grad_theirs = head_grads(query_in[0], grad_out[0], out_weight, members)
    parts = [sends[0]] + [swap(sends[mask], "seq", mask) for mask in range(1, members)]
    grad_mine, grad_theirs, *parts[1:2] = after(grad_mine, grad_theirs, *parts[1:2])
    half_grads = [grad_mine] + [
        swap(grad_theirs if mask & 1 else grad_mine, "seq", mask) for mask in range(1, members)
    ]

    near, norm = forward(bias, pairs, parts, scale)
    near_pair = swap(near, "seq", 1)
    returns, *sends = backward(bias, norm, pairs, parts, near, scale)
    near, returns = after(near, returns)
    returned = lax.all_to_all(returns, "seq", split_axis=0, concat_axis=0, tiled=True)
    parts = [sends[0]] + [swap(sends[mask], "seq", mask) for mask in range(1, members)]

    own, send = weight_parts(near, near_pair, half_grads, rep_count)
    bit = 1
    while 2 * bit < rep_count:
        own, send = weight_fold(own, swap(send, "rep", bit))
        bit *= 2
    own, *sends = weight_spread(own, swap(send, "rep", bit))
    arrived = [swap(block, "seq", mask) for block, mask in zip(sends, (members, 1, members + 1))]
    mixed_out, token = project(join_heads(parts), out_weight)
    factor = 1.0 / math.sqrt(rep_count * tokens)
    pair = weight_scale(token, own, *arrived, factor)
    query_grad, key_grad, value_grad, token = unpack(
        returned, parts, tokens_here, query_in.shape[2]
    )
    across, token = after(swap(pair, "rep", 2), token)
    quarters = [pair, swap(pair, "rep", 1), across, swap(across, "rep", 1)]
    weight_grad = weight_join(token, quarters)
    return (mixed_out[None], query_grad[None], key_grad[None], value_grad[None], weight_grad)


    return (mixed_out[None], query_grad[None], key_grad[None], value_grad[None], weight_grad)


    return (mixed_out[None], query_grad[None], key_grad[None], value_grad[None], weight_grad)


def local(query_in, key_in, value_in, out_weight, grad_out, pattern):
    seq_count, rep_count = lax.axis_size("seq"), lax.axis_size("rep")
    one_head_each = seq_count * HD == query_in.shape[2] and query_in.shape[0] == 1
    paired = seq_count & (seq_count - 1) == 0 and rep_count == 4
    if one_head_each and paired and seq_count > 2:
        return dense_local(query_in, key_in, value_in, out_weight, grad_out, pattern)
    return general_local(query_in, key_in, value_in, out_weight, grad_out, pattern)


def general_local(query_in, key_in, value_in, out_weight, grad_out, pattern):
    seq_count = lax.axis_size("seq")
    rep_count = lax.axis_size("rep")
    tokens_here = query_in.shape[1]
    width = query_in.shape[2]
    head_size = HD
    head_count = width // head_size
    groups = max(seq_count // head_count, 1)
    per_device = max(head_count // seq_count, 1)
    head_groups = head_count // per_device
    local_blocks = tokens_here // BLK
    group_rows = BLK // groups
    all_blocks = seq_count * local_blocks
    columns = per_device * head_size
    span = pattern.shape[1]
    block_run = math.gcd(all_blocks, 32)
    run_count = all_blocks // block_run
    scale = 1.0 / math.sqrt(head_size)

    def to_heads(source):
        shaped = source.reshape(local_blocks, groups, group_rows, head_groups, columns)
        return shaped.transpose(3, 1, 0, 2, 4).reshape(
            seq_count, local_blocks * group_rows, columns
        )

    def to_tokens(source):
        shaped = source.reshape(head_groups, groups, local_blocks, group_rows, columns)
        return shaped.transpose(2, 1, 3, 0, 4).reshape(tokens_here, width)

    query_local = query_in[0]
    key_local = key_in[0]
    value_local = value_in[0]
    grad_local = grad_out[0]

    def spread(source):
        grouped = source.reshape(tokens_here, head_groups, columns).transpose(1, 0, 2)
        copies = jnp.broadcast_to(grouped[:, None], (head_groups, groups, tokens_here, columns))
        return copies.reshape(seq_count, tokens_here, columns)

    query_heads, key_all, value_all = (
        lax.all_to_all(to_heads(query_local), "seq", split_axis=0, concat_axis=0, tiled=True),
        lax.all_to_all(spread(key_local), "seq", split_axis=0, concat_axis=0, tiled=True),
        lax.all_to_all(spread(value_local), "seq", split_axis=0, concat_axis=0, tiled=True),
    )
    attended_grad = lax.dot_general(
        grad_local, out_weight, (((1,), (1,)), ((), ())), preferred_element_type=jnp.float32
    ).astype(jnp.bfloat16)
    grad_heads = lax.all_to_all(
        to_heads(attended_grad), "seq", split_axis=0, concat_axis=0, tiled=True
    )
    key_blocks = key_all.reshape(all_blocks, BLK, per_device, head_size)
    value_blocks = value_all.reshape(all_blocks, BLK, per_device, head_size)
    query_runs = query_heads.reshape(run_count, block_run, group_rows, per_device, head_size)
    grad_runs = grad_heads.reshape(run_count, block_run, group_rows, per_device, head_size)
    pattern_runs = pattern.reshape(run_count, block_run, span)

    def attend_step(carry, items):
        key_acc, value_acc = carry
        query_run, grad_run, pattern_run = items
        key_gathered = key_blocks[pattern_run].reshape(block_run, span * BLK, per_device, head_size)
        value_gathered = value_blocks[pattern_run].reshape(
            block_run, span * BLK, per_device, head_size
        )
        scores = (
            jnp.einsum(
                "crhd,ckhd->chrk", query_run, key_gathered, preferred_element_type=jnp.float32
            )
            * scale
        )
        shifted = scores - jnp.max(scores, axis=-1, keepdims=True)
        weights = jnp.exp(shifted)
        probs = weights / jnp.sum(weights, axis=-1, keepdims=True)
        probs_low = probs.astype(jnp.bfloat16)
        result = jnp.einsum(
            "chrk,ckhd->crhd", probs_low, value_gathered, preferred_element_type=jnp.float32
        ).astype(jnp.bfloat16)
        prob_grad = jnp.einsum(
            "crhd,ckhd->chrk", grad_run, value_gathered, preferred_element_type=jnp.float32
        )
        delta = jnp.sum(probs * prob_grad, axis=-1, keepdims=True)
        score_grad = (probs * (prob_grad - delta)).astype(jnp.bfloat16)
        query_part = (
            jnp.einsum(
                "chrk,ckhd->crhd", score_grad, key_gathered, preferred_element_type=jnp.float32
            )
            * scale
        ).astype(jnp.bfloat16)
        key_contrib = (
            jnp.einsum("chrk,crhd->ckhd", score_grad, query_run, preferred_element_type=jnp.float32)
            * scale
        )
        value_contrib = jnp.einsum(
            "chrk,crhd->ckhd", probs_low, grad_run, preferred_element_type=jnp.float32
        )
        key_acc = key_acc.at[pattern_run].add(
            key_contrib.reshape(block_run, span, BLK, per_device, head_size)
        )
        value_acc = value_acc.at[pattern_run].add(
            value_contrib.reshape(block_run, span, BLK, per_device, head_size)
        )
        return ((key_acc, value_acc), (result, query_part))

    zero_grads = jnp.zeros((all_blocks, BLK, per_device, head_size), jnp.float32)
    (key_acc, value_acc), (out_heads, query_parts) = lax.scan(
        attend_step, (zero_grads, zero_grads), (query_runs, grad_runs, pattern_runs)
    )
    out_send = out_heads.reshape(seq_count, local_blocks * group_rows, columns)
    attended = to_tokens(lax.all_to_all(out_send, "seq", split_axis=0, concat_axis=0, tiled=True))
    mixed_out = jnp.dot(attended, out_weight, preferred_element_type=jnp.float32).astype(
        jnp.bfloat16
    )
    norm_factor = 1.0 / math.sqrt(rep_count * seq_count * tokens_here)
    weight_shard = lax.psum_scatter(
        lax.dot_general(
            attended, grad_local, (((0,), (0,)), ((), ())), preferred_element_type=jnp.float32
        ),
        ("seq", "rep"),
        scatter_dimension=0,
        tiled=True,
    )
    weight_grad = lax.all_gather(
        (weight_shard * norm_factor).astype(jnp.bfloat16), "rep", axis=0, tiled=True
    ).astype(jnp.float32)
    query_send = query_parts.reshape(seq_count, local_blocks * group_rows, columns)
    key_send = key_acc.astype(jnp.bfloat16).reshape(seq_count, tokens_here, columns)
    value_send = value_acc.astype(jnp.bfloat16).reshape(seq_count, tokens_here, columns)
    query_back, key_back, value_back = (
        lax.all_to_all(query_send, "seq", split_axis=0, concat_axis=0, tiled=True),
        lax.all_to_all(key_send, "seq", split_axis=0, concat_axis=0, tiled=True),
        lax.all_to_all(value_send, "seq", split_axis=0, concat_axis=0, tiled=True),
    )

    def fold_groups(source):
        summed = jnp.sum(
            source.reshape(head_groups, groups, tokens_here, columns).astype(jnp.float32), axis=1
        )
        return summed.astype(jnp.bfloat16).transpose(1, 0, 2).reshape(tokens_here, width)

    query_grad = to_tokens(query_back)
    key_grad = fold_groups(key_back)
    value_grad = fold_groups(value_back)
    return (mixed_out[None], query_grad[None], key_grad[None], value_grad[None], weight_grad)


def solution(mesh):
    placed = (
        P("rep", "seq", None),
        P("rep", "seq", None),
        P("rep", "seq", None),
        P(),
        P("rep", "seq", None),
        P(),
    )
    return jax.shard_map(
        local,
        mesh=mesh,
        in_specs=placed,
        out_specs=(
            P("rep", "seq", None),
            P("rep", "seq", None),
            P("rep", "seq", None),
            P("rep", "seq", None),
            P("seq", None),
        ),
        check_vma=False,
    )
```

```python
import functools
import math

import jax
import jax.numpy as jnp
from jax import lax
from jax.experimental import pallas as pl
from jax.experimental.pallas import tpu as pltpu
from jax.sharding import PartitionSpec as P

HD = 128
BLK = 64
MASKED = -1e30
LOG2E = math.log2(math.e)
VMEM = pltpu.VMEM
ANY_SPEC = pl.BlockSpec(memory_space=pl.ANY)
VMEM_SPEC = pl.BlockSpec()
NT = (((1,), (1,)), ((), ()))
NN = (((1,), (0,)), ((), ()))
WIDE = 58
HEAD_MIB = 58
PROJECT_FLOPS = 1
SCALE_FLOPS = 8 << 30
HEADS_FLOPS = 1


def dot(left, right, dims):
    return lax.dot_general(left, right, dims, preferred_element_type=jnp.float32)


def params(mib):
    return pltpu.CompilerParams(vmem_limit_bytes=mib * 1024 * 1024)


def cost(flops=1, moved=1):
    return pl.CostEstimate(flops=flops, bytes_accessed=moved, transcendentals=0)


def struct(*shape, dtype=jnp.bfloat16):
    return jax.ShapeDtypeStruct(shape, dtype)


def in_hbm(array):
    return pltpu.with_memory_space_constraint(array, pltpu.HBM)


def span(index, size):
    return pl.ds(pl.multiple_of(index * size, size), size)


def swap(array, axis, mask):
    return lax.ppermute(array, axis, [(i, i ^ mask) for i in range(lax.axis_size(axis))])


def after(*arrays):
    return lax.optimization_barrier(arrays)


def anchored(kernel):
    return lambda anchor, *refs: kernel(*refs)


def members_of(peers):
    return peers // 2


def member(mask=0):
    return (lax.axis_index("seq") ^ mask) & (members_of(lax.axis_size("seq")) - 1)


def half_of():
    return lax.axis_index("seq") // members_of(lax.axis_size("seq"))


def pack_kernel(key_ref, value_ref, send, *refs):
    held, sem = refs[:2], refs[2]
    rows, width = key_ref.shape
    peers = send.shape[0]
    loads = [
        pltpu.make_async_copy(source, target, sem.at[index])
        for index, (source, target) in enumerate(zip((key_ref, value_ref), held))
    ]
    for load in loads:
        load.start()
    for index, source in enumerate(held):
        loads[index].wait()
        for peer in range(peers):
            for slot in range(2):
                head = peer % members_of(peers) + slot * members_of(peers)
                place = pl.ds((2 * index + slot) * rows, rows)
                send[peer, place] = source[:, head * HD : (head + 1) * HD]


def pack(keys, values, peers):
    rows, width = keys.shape
    return pl.pallas_call(
        pack_kernel,
        out_shape=struct(peers, 4 * rows, HD),
        in_specs=[ANY_SPEC] * 2,
        out_specs=VMEM_SPEC,
        scratch_shapes=[VMEM((rows, width), jnp.bfloat16)] * 2 + [pltpu.SemaphoreType.DMA((2,))],
        compiler_params=params(WIDE),
        cost_estimate=cost(),
        name="pack_keys",
    )(keys, values)


def head_grad_kernel(query_ref, grad_ref, weight_ref, *refs):
    sends, (mine, theirs), refs = refs[:-7], refs[-7:-5], refs[-5:]
    query, grad, weight, head_grad, sem = refs
    rows = query_ref.shape[0]
    members = len(sends)
    loads = [
        pltpu.make_async_copy(source, target, sem.at[index])
        for index, (source, target) in enumerate(
            zip((query_ref, grad_ref, weight_ref), (query, grad, weight))
        )
    ]
    for load in loads:
        load.start()
    loads[0].wait()
    for mask, send in enumerate(sends):
        for slot in range(2):
            send[slot * rows : (slot + 1) * rows] = query[:, span(member(mask) + slot * members, HD)]
    loads[1].wait()
    side = lax.axis_index("seq") & 1
    mine[...] = grad[:, span(side, mine.shape[1])]
    theirs[...] = grad[:, span(1 - side, theirs.shape[1])]
    loads[2].wait()
    head_grad[...] = dot(weight[...], grad[...], NT).astype(jnp.bfloat16)
    for mask, send in enumerate(sends):
        for slot in range(2):
            place = pl.ds(2 * rows + slot * HD, HD)
            send[place] = head_grad[span(member(mask) + slot * members, HD)]


def head_grads(queries, grads, out_weight, members):
    rows, width = queries.shape
    return pl.pallas_call(
        head_grad_kernel,
        out_shape=[pltpu.HBM((2 * rows + 2 * HD, HD), jnp.bfloat16)] * members
        + [pltpu.HBM((rows, grads.shape[1] // 2), jnp.bfloat16)] * 2,
        in_specs=[ANY_SPEC] * 3,
        out_specs=[VMEM_SPEC] * (members + 2),
        scratch_shapes=[
            VMEM(queries.shape, jnp.bfloat16),
            VMEM(grads.shape, jnp.bfloat16),
            VMEM(out_weight.shape, jnp.bfloat16),
            VMEM((width, rows), jnp.bfloat16),
            pltpu.SemaphoreType.DMA((3,)),
        ],
        compiler_params=params(HEAD_MIB),
        cost_estimate=cost(),
        name="head_grads",
    )(queries, grads, out_weight)


def load_queries(parts, queries, grads=None):
    rows = parts[0].shape[0] // 4
    for mask, part in enumerate(parts):
        for slot in range(2):
            queries[slot, span(member(mask), rows)] = part[slot * rows : (slot + 1) * rows]
            if grads is not None:
                grad = part[2 * rows + slot * HD : 2 * rows + (slot + 1) * HD]
                grads[slot, :, span(member(mask), rows)] = grad


def load_heads(pairs, keys, values):
    rows = pairs.shape[1] // 4
    for peer in range(pairs.shape[0]):
        for slot in range(2):
            place = slice(peer * rows, (peer + 1) * rows)
            keys[slot, place] = pairs[peer, slot * rows : (slot + 1) * rows]
            values[slot, place] = pairs[peer, (2 + slot) * rows : (3 + slot) * rows]


def scores_of(keys, queries, bias, scale):
    blocks = bias.shape[0]
    scores = dot(keys, queries, NT) * (scale * LOG2E)
    shaped = scores.reshape(blocks, BLK, queries.shape[0]) + bias[:, None, :]
    return shaped.reshape(scores.shape)


def forward_kernel(members, chunk, scale, bias_ref, pairs, *refs):
    parts, (near, norm_ref, keys, values, queries) = refs[:members], refs[members:]
    load_heads(pairs, keys, values)
    load_queries(parts, queries)
    tokens = queries.shape[1]
    for slot in range(2):
        value_cols = values[slot].T
        for step in range(tokens // chunk):
            rows = slice(step * chunk, (step + 1) * chunk)
            bias = bias_ref[:, span(half_of() * (tokens // chunk) + step, chunk)]
            scores = scores_of(keys[slot], queries[slot, rows], bias, scale)
            top = jnp.max(scores, axis=0, keepdims=True)
            weights = jnp.exp2(scores - top)
            total = jnp.sum(weights, axis=0, keepdims=True)
            probs_low = (weights * (1.0 / total)).astype(jnp.bfloat16)
            place = pl.ds(slot * tokens + step * chunk, chunk)
            near[place] = dot(value_cols, probs_low, NN).T.astype(jnp.bfloat16)
            norm_ref[slot : slot + 1, rows] = top + jnp.log2(total)


def forward(bias, pairs, parts, scale):
    tokens = bias.shape[1]
    chunk = 4 * tokens // pairs.shape[0]
    stats = struct(2, tokens // 2, dtype=jnp.float32)
    return pl.pallas_call(
        functools.partial(forward_kernel, len(parts), chunk, scale),
        out_shape=[struct(tokens, HD), stats],
        in_specs=[VMEM_SPEC] * (2 + len(parts)),
        out_specs=[VMEM_SPEC] * 2,
        scratch_shapes=[VMEM((2, tokens, HD), jnp.bfloat16)] * 2
        + [VMEM((2, tokens // 2, HD), jnp.bfloat16)],
        compiler_params=params(30),
        cost_estimate=cost(),
        name="attend",
    )(bias, pairs, *parts)


def backward_kernel(members, chunk, scale, bias_ref, norm_ref, pairs, near, *refs):
    parts, returns, outs, refs = refs[:members], refs[members], refs[members + 1 : -5], refs[-5:]
    keys, values, queries, grads, query_grad = refs
    load_heads(pairs, keys, values)
    load_queries(parts, queries, grads)
    tokens = queries.shape[1]
    peers = returns.shape[0]
    here = returns.shape[1] // 4
    for slot in range(2):
        key_cols = keys[slot].T
        for step in range(tokens // chunk):
            rows = slice(step * chunk, (step + 1) * chunk)
            bias = bias_ref[:, span(half_of() * (tokens // chunk) + step, chunk)]
            bias = bias - norm_ref[slot : slot + 1, rows]
            probs = jnp.exp2(scores_of(keys[slot], queries[slot, rows], bias, scale))
            prob_grad = dot(values[slot], grads[slot, :, rows], NN)
            delta = jnp.sum(probs * prob_grad, axis=0, keepdims=True)
            score_grad = (probs * (prob_grad - delta)).astype(jnp.bfloat16)
            value_part = dot(probs.astype(jnp.bfloat16), grads[slot, :, rows], NT)
            key_part = dot(score_grad, queries[slot, rows], NN)
            key_total = key_part if step == 0 else key_total + key_part
            value_total = value_part if step == 0 else value_total + value_part
            query_part = dot(key_cols, score_grad, NN) * scale
            query_grad[slot, rows] = query_part.T.astype(jnp.bfloat16)
        for first, total in ((slot, key_total * scale), (2 + slot, value_total)):
            low = total.astype(jnp.bfloat16).reshape(peers, here, HD)
            returns[:, first * here : (first + 1) * here] = low
        for mask, out in enumerate(outs):
            theirs = span(member(mask), here)
            out[slot * here : (slot + 1) * here] = query_grad[slot, theirs]
            theirs = span(slot * len(outs) + member(mask), here)
            out[(2 + slot) * here : (3 + slot) * here] = near[theirs]


def backward(bias, norm, pairs, parts, near, scale):
    peers, tokens = pairs.shape[0], bias.shape[1]
    members = members_of(peers)
    here = tokens // peers
    return pl.pallas_call(
        functools.partial(backward_kernel, members, 4 * here, scale),
        out_shape=[struct(peers, 4 * here, HD)] + [pltpu.HBM((4 * here, HD), jnp.bfloat16)] * members,
        in_specs=[VMEM_SPEC] * (4 + members),
        out_specs=[VMEM_SPEC] * (1 + members),
        scratch_shapes=[VMEM((2, tokens, HD), jnp.bfloat16)] * 2
        + [VMEM((2, tokens // 2, HD), jnp.bfloat16), VMEM((2, HD, tokens // 2), jnp.bfloat16)]
        + [VMEM((2, tokens // 2, HD), jnp.bfloat16)],
        compiler_params=params(30),
        cost_estimate=cost(),
        name="attend_back",
    )(bias, norm, pairs, near, *parts)


def unpack_kernel(returned, *refs):
    queries, (query_grad, key_grad, value_grad, token) = refs[:-4], refs[-4:]
    token[...] = jnp.zeros_like(token)
    members = len(queries)
    here = query_grad.shape[0]
    for index in range(members):
        for slot in range(2):
            columns = pl.ds((index + slot * members) * HD, HD)
            for target, first in ((key_grad, slot), (value_grad, 2 + slot)):
                rows = slice(first * here, (first + 1) * here)
                both = returned[index, rows].astype(jnp.float32) + returned[
                    index + members, rows
                ].astype(jnp.float32)
                target[:, columns] = both.astype(jnp.bfloat16)
            part = queries[index][slot * here : (slot + 1) * here]
            query_grad[:, span(member(index) + slot * members, HD)] = part


def unpack(returned, queries, rows, width):
    return pl.pallas_call(
        unpack_kernel,
        out_shape=[struct(rows, width)] * 3 + [struct(16, HD)],
        in_specs=[VMEM_SPEC] * (1 + len(queries)),
        out_specs=[VMEM_SPEC] * 4,
        compiler_params=params(16),
        cost_estimate=cost(1, 24 * rows * width),
        name="unpack_grads",
    )(returned, *map(in_hbm, queries))


def join_heads_kernel(*refs):
    parts, attended = refs[:-1], refs[-1]
    rows = attended.shape[0]
    for mask, part in enumerate(parts):
        for slot in range(2):
            columns = span(member(mask) + slot * len(parts), HD)
            attended[:, columns] = part[(2 + slot) * rows : (3 + slot) * rows]


def join_heads(parts):
    rows = parts[0].shape[0] // 4
    return pl.pallas_call(
        join_heads_kernel,
        out_shape=struct(rows, 2 * HD * len(parts)),
        in_specs=[VMEM_SPEC] * len(parts),
        out_specs=VMEM_SPEC,
        compiler_params=params(8),
        cost_estimate=cost(HEADS_FLOPS),
        name="join_heads",
    )(*map(in_hbm, parts))


def project_kernel(attended, weight_ref, out_ref, token):
    token[...] = jnp.zeros_like(token)
    out_ref[...] = dot(attended[...], weight_ref[...], NN).astype(jnp.bfloat16)


def project(attended, out_weight):
    rows = attended.shape[0]
    depth, width = out_weight.shape
    tile = width // 4
    return pl.pallas_call(
        project_kernel,
        out_shape=[struct(rows, width), struct(16, HD)],
        grid=(width // tile,),
        in_specs=[
            pl.BlockSpec((rows, depth), lambda i: (0, 0)),
            pl.BlockSpec((depth, tile), lambda i: (0, i)),
        ],
        out_specs=[
            pl.BlockSpec((rows, tile), lambda i: (0, i)),
            pl.BlockSpec((16, HD), lambda i: (0, 0)),
        ],
        compiler_params=params(30),
        cost_estimate=cost(PROJECT_FLOPS, 1),
        name="project",
    )(attended, out_weight)


def weight_part_kernel(masks, docs, near, near_pair, *refs):
    grads, out = refs[:-1], refs[-1]
    members = len(grads)
    rows = grads[0].shape[0]
    width = grads[0].shape[1] // docs
    lefts = []
    for source in (near, near_pair):
        for slot in range(2):
            places = [span(slot * members + member(mask), rows) for mask in range(members)]
            lefts.append(jnp.concatenate([source[place] for place in places], axis=0))
    left = jnp.concatenate(lefts, axis=1).T
    for index, mask in enumerate(masks):
        columns = span(lax.axis_index("rep") ^ mask, width)
        right = jnp.concatenate([grad[:, columns] for grad in grads], axis=0)
        place = pl.ds(index * left.shape[0], left.shape[0])
        out[place] = dot(left, right, NN).astype(out.dtype)


def weight_part(near, near_pair, grads, docs, first, dtype):
    masks = range(first, docs, 2)
    width = grads[0].shape[1] // docs
    return pl.pallas_call(
        functools.partial(weight_part_kernel, masks, docs),
        out_shape=struct(len(masks) * 4 * HD, width, dtype=dtype),
        in_specs=[VMEM_SPEC] * (2 + len(grads)),
        out_specs=VMEM_SPEC,
        compiler_params=params(24),
        cost_estimate=cost(),
        name="weight_part",
    )(near, near_pair, *map(in_hbm, grads))


def weight_fold_kernel(own, other, keep, send):
    rows = keep.shape[0]
    keep[...] = own[:rows] + other[:rows].astype(jnp.float32)
    send[...] = (own[rows:] + other[rows:].astype(jnp.float32)).astype(jnp.bfloat16)


def weight_fold(own, other):
    rows, width = own.shape
    return pl.pallas_call(
        weight_fold_kernel,
        out_shape=[struct(rows // 2, width, dtype=jnp.float32), struct(rows // 2, width)],
        in_specs=[VMEM_SPEC] * 2,
        out_specs=[VMEM_SPEC] * 2,
        compiler_params=params(8),
        cost_estimate=cost(),
        name="weight_fold",
    )(own, other)


def weight_spread_kernel(own, other, *targets):
    rows = targets[0].shape[0]
    half = half_of()
    for index, target in enumerate(targets):
        block = span(index // 2 * 2 + (1 - half if index % 2 else half), rows)
        target[...] = (own[block] + other[block].astype(jnp.float32)).astype(target.dtype)


def weight_spread(own, other):
    rows, width = own.shape
    return pl.pallas_call(
        weight_spread_kernel,
        out_shape=[struct(rows // 4, width, dtype=jnp.float32)] + [struct(rows // 4, width)] * 3,
        in_specs=[VMEM_SPEC] * 2,
        out_specs=[VMEM_SPEC] * 4,
        compiler_params=params(8),
        cost_estimate=cost(),
        name="weight_spread",
    )(own, other)


def weight_scale_kernel(factor, first, second, total):
    wide = first[...].astype(jnp.float32) + second[...].astype(jnp.float32)
    total[...] = (wide * factor).astype(jnp.bfloat16)


def weight_scale(anchor, first, second, factor, flops):
    return pl.pallas_call(
        anchored(functools.partial(weight_scale_kernel, factor)),
        out_shape=struct(*first.shape),
        in_specs=[ANY_SPEC] + [VMEM_SPEC] * 2,
        out_specs=VMEM_SPEC,
        compiler_params=params(8),
        cost_estimate=cost(flops),
        name="weight_scale",
    )(anchor, first, second)


def weight_join_kernel(*refs):
    parts, total = refs[:-1], refs[-1]
    width = parts[0].shape[1]
    count = len(parts) // 2
    side = lax.axis_index("seq") & 1
    for index, part in enumerate(parts):
        share = lax.axis_index("rep") ^ (index % count)
        place = side if index < count else 1 - side
        total[:, span(place * count + share, width)] = part[...].astype(jnp.float32)


def weight_join(anchor, parts):
    rows, width = parts[0].shape
    return pl.pallas_call(
        anchored(weight_join_kernel),
        out_shape=struct(rows, width * len(parts), dtype=jnp.float32),
        in_specs=[ANY_SPEC] + [VMEM_SPEC] * len(parts),
        out_specs=VMEM_SPEC,
        compiler_params=params(8),
        cost_estimate=cost(),
        name="weight_join",
    )(anchor, *parts)


def dense_bias(pattern, tokens):
    blocks = pattern.shape[0]
    named = pattern[:, :, None] == jnp.arange(blocks, dtype=pattern.dtype)
    counts = jnp.sum(named.astype(jnp.float32), axis=1).T
    bias = jnp.where(counts > 0, jnp.log2(jnp.maximum(counts, 1.0)), MASKED)
    return jnp.repeat(bias, tokens // blocks, axis=1)


def dense_local(query_in, key_in, value_in, out_weight, grad_out, pattern):
    seq_count, rep_count = lax.axis_size("seq"), lax.axis_size("rep")
    tokens_here = query_in.shape[1]
    tokens = tokens_here * seq_count
    members = members_of(seq_count)
    scale = 1.0 / math.sqrt(HD)
    bias = dense_bias(pattern, tokens)

    pairs = lax.all_to_all(
        pack(key_in[0], value_in[0], seq_count), "seq", split_axis=0, concat_axis=0, tiled=True
    )
    *sends, grad_mine, grad_theirs = head_grads(query_in[0], grad_out[0], out_weight, members)
    parts = [sends[0]] + [swap(sends[mask], "seq", mask) for mask in range(1, members)]
    grad_mine, grad_theirs, *parts[1:2] = after(grad_mine, grad_theirs, *parts[1:2])
    half_grads = {1: swap(grad_theirs, "seq", 1)}
    grad_mine, grad_theirs, *parts[2:3] = after(grad_mine, grad_theirs, *parts[2:3])
    half_grads |= {
        mask: swap(grad_theirs if mask & 1 else grad_mine, "seq", mask) for mask in range(2, members)
    }
    half_grads = [grad_mine] + [half_grads[mask] for mask in range(1, members)]

    near, norm = forward(bias, pairs, parts, scale)
    near_pair = swap(near, "seq", 1)
    returns, *sends = backward(bias, norm, pairs, parts, near, scale)
    near, returns = after(near, returns)
    returned = lax.all_to_all(returns, "seq", split_axis=0, concat_axis=0, tiled=True)
    parts = [sends[0]] + [swap(sends[mask], "seq", mask) for mask in range(1, members)]

    send = weight_part(near, near_pair, half_grads, rep_count, 1, jnp.bfloat16)
    own = weight_part(near, near_pair, half_grads, rep_count, 0, jnp.float32)
    bit = 1
    while 2 * bit < rep_count:
        own, send = weight_fold(own, swap(send, "rep", bit))
        bit *= 2
    own, *sends = weight_spread(own, swap(send, "rep", bit))
    arrived = [swap(block, "seq", mask) for block, mask in zip(sends, (members, 1, members + 1))]
    mixed_out, token = project(join_heads(parts), out_weight)
    factor = 1.0 / math.sqrt(rep_count * tokens)
    mine = weight_scale(token, own, arrived[0], factor, 1)
    other = weight_scale(token, arrived[1], arrived[2], factor, SCALE_FLOPS)
    query_grad, key_grad, value_grad, token = unpack(
        returned, parts, tokens_here, query_in.shape[2]
    )
    shares = []
    for share in (mine, other):
        across, token = after(swap(share, "rep", 2), token)
        shares += [share, swap(share, "rep", 1), across, swap(across, "rep", 1)]
    weight_grad = weight_join(token, shares)
    return (mixed_out[None], query_grad[None], key_grad[None], value_grad[None], weight_grad)


    return (mixed_out[None], query_grad[None], key_grad[None], value_grad[None], weight_grad)


    return (mixed_out[None], query_grad[None], key_grad[None], value_grad[None], weight_grad)


def local(query_in, key_in, value_in, out_weight, grad_out, pattern):
    seq_count, rep_count = lax.axis_size("seq"), lax.axis_size("rep")
    one_head_each = seq_count * HD == query_in.shape[2] and query_in.shape[0] == 1
    paired = seq_count & (seq_count - 1) == 0 and rep_count == 4
    if one_head_each and paired and seq_count > 2:
        return dense_local(query_in, key_in, value_in, out_weight, grad_out, pattern)
    return general_local(query_in, key_in, value_in, out_weight, grad_out, pattern)


def general_local(query_in, key_in, value_in, out_weight, grad_out, pattern):
    seq_count = lax.axis_size("seq")
    rep_count = lax.axis_size("rep")
    tokens_here = query_in.shape[1]
    width = query_in.shape[2]
    head_size = HD
    head_count = width // head_size
    groups = max(seq_count // head_count, 1)
    per_device = max(head_count // seq_count, 1)
    head_groups = head_count // per_device
    local_blocks = tokens_here // BLK
    group_rows = BLK // groups
    all_blocks = seq_count * local_blocks
    columns = per_device * head_size
    span = pattern.shape[1]
    block_run = math.gcd(all_blocks, 32)
    run_count = all_blocks // block_run
    scale = 1.0 / math.sqrt(head_size)

    def to_heads(source):
        shaped = source.reshape(local_blocks, groups, group_rows, head_groups, columns)
        return shaped.transpose(3, 1, 0, 2, 4).reshape(
            seq_count, local_blocks * group_rows, columns
        )

    def to_tokens(source):
        shaped = source.reshape(head_groups, groups, local_blocks, group_rows, columns)
        return shaped.transpose(2, 1, 3, 0, 4).reshape(tokens_here, width)

    query_local = query_in[0]
    key_local = key_in[0]
    value_local = value_in[0]
    grad_local = grad_out[0]

    def spread(source):
        grouped = source.reshape(tokens_here, head_groups, columns).transpose(1, 0, 2)
        copies = jnp.broadcast_to(grouped[:, None], (head_groups, groups, tokens_here, columns))
        return copies.reshape(seq_count, tokens_here, columns)

    query_heads, key_all, value_all = (
        lax.all_to_all(to_heads(query_local), "seq", split_axis=0, concat_axis=0, tiled=True),
        lax.all_to_all(spread(key_local), "seq", split_axis=0, concat_axis=0, tiled=True),
        lax.all_to_all(spread(value_local), "seq", split_axis=0, concat_axis=0, tiled=True),
    )
    attended_grad = lax.dot_general(
        grad_local, out_weight, (((1,), (1,)), ((), ())), preferred_element_type=jnp.float32
    ).astype(jnp.bfloat16)
    grad_heads = lax.all_to_all(
        to_heads(attended_grad), "seq", split_axis=0, concat_axis=0, tiled=True
    )
    key_blocks = key_all.reshape(all_blocks, BLK, per_device, head_size)
    value_blocks = value_all.reshape(all_blocks, BLK, per_device, head_size)
    query_runs = query_heads.reshape(run_count, block_run, group_rows, per_device, head_size)
    grad_runs = grad_heads.reshape(run_count, block_run, group_rows, per_device, head_size)
    pattern_runs = pattern.reshape(run_count, block_run, span)

    def attend_step(carry, items):
        key_acc, value_acc = carry
        query_run, grad_run, pattern_run = items
        key_gathered = key_blocks[pattern_run].reshape(block_run, span * BLK, per_device, head_size)
        value_gathered = value_blocks[pattern_run].reshape(
            block_run, span * BLK, per_device, head_size
        )
        scores = (
            jnp.einsum(
                "crhd,ckhd->chrk", query_run, key_gathered, preferred_element_type=jnp.float32
            )
            * scale
        )
        shifted = scores - jnp.max(scores, axis=-1, keepdims=True)
        weights = jnp.exp(shifted)
        probs = weights / jnp.sum(weights, axis=-1, keepdims=True)
        probs_low = probs.astype(jnp.bfloat16)
        result = jnp.einsum(
            "chrk,ckhd->crhd", probs_low, value_gathered, preferred_element_type=jnp.float32
        ).astype(jnp.bfloat16)
        prob_grad = jnp.einsum(
            "crhd,ckhd->chrk", grad_run, value_gathered, preferred_element_type=jnp.float32
        )
        delta = jnp.sum(probs * prob_grad, axis=-1, keepdims=True)
        score_grad = (probs * (prob_grad - delta)).astype(jnp.bfloat16)
        query_part = (
            jnp.einsum(
                "chrk,ckhd->crhd", score_grad, key_gathered, preferred_element_type=jnp.float32
            )
            * scale
        ).astype(jnp.bfloat16)
        key_contrib = (
            jnp.einsum("chrk,crhd->ckhd", score_grad, query_run, preferred_element_type=jnp.float32)
            * scale
        )
        value_contrib = jnp.einsum(
            "chrk,crhd->ckhd", probs_low, grad_run, preferred_element_type=jnp.float32
        )
        key_acc = key_acc.at[pattern_run].add(
            key_contrib.reshape(block_run, span, BLK, per_device, head_size)
        )
        value_acc = value_acc.at[pattern_run].add(
            value_contrib.reshape(block_run, span, BLK, per_device, head_size)
        )
        return ((key_acc, value_acc), (result, query_part))

    zero_grads = jnp.zeros((all_blocks, BLK, per_device, head_size), jnp.float32)
    (key_acc, value_acc), (out_heads, query_parts) = lax.scan(
        attend_step, (zero_grads, zero_grads), (query_runs, grad_runs, pattern_runs)
    )
    out_send = out_heads.reshape(seq_count, local_blocks * group_rows, columns)
    attended = to_tokens(lax.all_to_all(out_send, "seq", split_axis=0, concat_axis=0, tiled=True))
    mixed_out = jnp.dot(attended, out_weight, preferred_element_type=jnp.float32).astype(
        jnp.bfloat16
    )
    norm_factor = 1.0 / math.sqrt(rep_count * seq_count * tokens_here)
    weight_shard = lax.psum_scatter(
        lax.dot_general(
            attended, grad_local, (((0,), (0,)), ((), ())), preferred_element_type=jnp.float32
        ),
        ("seq", "rep"),
        scatter_dimension=0,
        tiled=True,
    )
    weight_grad = lax.all_gather(
        (weight_shard * norm_factor).astype(jnp.bfloat16), "rep", axis=0, tiled=True
    ).astype(jnp.float32)
    query_send = query_parts.reshape(seq_count, local_blocks * group_rows, columns)
    key_send = key_acc.astype(jnp.bfloat16).reshape(seq_count, tokens_here, columns)
    value_send = value_acc.astype(jnp.bfloat16).reshape(seq_count, tokens_here, columns)
    query_back, key_back, value_back = (
        lax.all_to_all(query_send, "seq", split_axis=0, concat_axis=0, tiled=True),
        lax.all_to_all(key_send, "seq", split_axis=0, concat_axis=0, tiled=True),
        lax.all_to_all(value_send, "seq", split_axis=0, concat_axis=0, tiled=True),
    )

    def fold_groups(source):
        summed = jnp.sum(
            source.reshape(head_groups, groups, tokens_here, columns).astype(jnp.float32), axis=1
        )
        return summed.astype(jnp.bfloat16).transpose(1, 0, 2).reshape(tokens_here, width)

    query_grad = to_tokens(query_back)
    key_grad = fold_groups(key_back)
    value_grad = fold_groups(value_back)
    return (mixed_out[None], query_grad[None], key_grad[None], value_grad[None], weight_grad)


def solution(mesh):
    placed = (
        P("rep", "seq", None),
        P("rep", "seq", None),
        P("rep", "seq", None),
        P(),
        P("rep", "seq", None),
        P(),
    )
    return jax.shard_map(
        local,
        mesh=mesh,
        in_specs=placed,
        out_specs=(
            P("rep", "seq", None),
            P("rep", "seq", None),
            P("rep", "seq", None),
            P("rep", "seq", None),
            P("seq", None),
        ),
        check_vma=False,
    )
```

```python
import functools
import math

import jax
import jax.numpy as jnp
from jax import lax
from jax.experimental import pallas as pl
from jax.experimental.pallas import tpu as pltpu
from jax.sharding import PartitionSpec as P

HD = 128
BLK = 64
MASKED = -1e30
LOG2E = math.log2(math.e)
VMEM = pltpu.VMEM
ANY_SPEC = pl.BlockSpec(memory_space=pl.ANY)
VMEM_SPEC = pl.BlockSpec()
NT = (((1,), (1,)), ((), ()))
NN = (((1,), (0,)), ((), ()))
WIDE = 58
HEAD_MIB = 58
PROJECT_FLOPS = 1
SCALE_FLOPS = 8 << 30
HEADS_FLOPS = 1


def dot(left, right, dims):
    return lax.dot_general(left, right, dims, preferred_element_type=jnp.float32)


def params(mib):
    return pltpu.CompilerParams(vmem_limit_bytes=mib * 1024 * 1024)


def cost(flops=1, moved=1):
    return pl.CostEstimate(flops=flops, bytes_accessed=moved, transcendentals=0)


def struct(*shape, dtype=jnp.bfloat16):
    return jax.ShapeDtypeStruct(shape, dtype)


def in_hbm(array):
    return pltpu.with_memory_space_constraint(array, pltpu.HBM)


def span(index, size):
    return pl.ds(pl.multiple_of(index * size, size), size)


def swap(array, axis, mask):
    return lax.ppermute(array, axis, [(i, i ^ mask) for i in range(lax.axis_size(axis))])


def after(*arrays):
    return lax.optimization_barrier(arrays)


def anchored(kernel):
    return lambda anchor, *refs: kernel(*refs)


def members_of(peers):
    return peers // 2


def member(mask=0):
    return (lax.axis_index("seq") ^ mask) & (members_of(lax.axis_size("seq")) - 1)


def half_of():
    return lax.axis_index("seq") // members_of(lax.axis_size("seq"))


def pack_kernel(key_ref, value_ref, send, *refs):
    held, sem = refs[:2], refs[2]
    rows, width = key_ref.shape
    peers = send.shape[0]
    loads = [
        pltpu.make_async_copy(source, target, sem.at[index])
        for index, (source, target) in enumerate(zip((key_ref, value_ref), held))
    ]
    for load in loads:
        load.start()
    for index, source in enumerate(held):
        loads[index].wait()
        for peer in range(peers):
            for slot in range(2):
                head = peer % members_of(peers) + slot * members_of(peers)
                place = pl.ds((2 * index + slot) * rows, rows)
                send[peer, place] = source[:, head * HD : (head + 1) * HD]


def pack(keys, values, peers):
    rows, width = keys.shape
    return pl.pallas_call(
        pack_kernel,
        out_shape=struct(peers, 4 * rows, HD),
        in_specs=[ANY_SPEC] * 2,
        out_specs=VMEM_SPEC,
        scratch_shapes=[VMEM((rows, width), jnp.bfloat16)] * 2 + [pltpu.SemaphoreType.DMA((2,))],
        compiler_params=params(WIDE),
        cost_estimate=cost(),
        name="pack_keys",
    )(keys, values)


def head_grad_kernel(query_ref, grad_ref, weight_ref, *refs):
    sends, (mine, theirs), refs = refs[:-7], refs[-7:-5], refs[-5:]
    query, grad, weight, head_grad, sem = refs
    rows = query_ref.shape[0]
    members = len(sends)
    loads = [
        pltpu.make_async_copy(source, target, sem.at[index])
        for index, (source, target) in enumerate(
            zip((query_ref, grad_ref, weight_ref), (query, grad, weight))
        )
    ]
    for load in loads:
        load.start()
    loads[0].wait()
    for mask, send in enumerate(sends):
        for slot in range(2):
            send[slot * rows : (slot + 1) * rows] = query[:, span(member(mask) + slot * members, HD)]
    loads[1].wait()
    side = lax.axis_index("seq") & 1
    mine[...] = grad[:, span(side, mine.shape[1])]
    theirs[...] = grad[:, span(1 - side, theirs.shape[1])]
    loads[2].wait()
    head_grad[...] = dot(weight[...], grad[...], NT).astype(jnp.bfloat16)
    for mask, send in enumerate(sends):
        for slot in range(2):
            place = pl.ds(2 * rows + slot * HD, HD)
            send[place] = head_grad[span(member(mask) + slot * members, HD)]


def head_grads(queries, grads, out_weight, members):
    rows, width = queries.shape
    return pl.pallas_call(
        head_grad_kernel,
        out_shape=[pltpu.HBM((2 * rows + 2 * HD, HD), jnp.bfloat16)] * members
        + [pltpu.HBM((rows, grads.shape[1] // 2), jnp.bfloat16)] * 2,
        in_specs=[ANY_SPEC] * 3,
        out_specs=[VMEM_SPEC] * (members + 2),
        scratch_shapes=[
            VMEM(queries.shape, jnp.bfloat16),
            VMEM(grads.shape, jnp.bfloat16),
            VMEM(out_weight.shape, jnp.bfloat16),
            VMEM((width, rows), jnp.bfloat16),
            pltpu.SemaphoreType.DMA((3,)),
        ],
        compiler_params=params(HEAD_MIB),
        cost_estimate=cost(),
        name="head_grads",
    )(queries, grads, out_weight)


def load_queries(parts, queries, grads=None):
    rows = parts[0].shape[0] // 4
    for mask, part in enumerate(parts):
        for slot in range(2):
            queries[slot, span(member(mask), rows)] = part[slot * rows : (slot + 1) * rows]
            if grads is not None:
                grad = part[2 * rows + slot * HD : 2 * rows + (slot + 1) * HD]
                grads[slot, :, span(member(mask), rows)] = grad


def load_heads(pairs, keys, values):
    rows = pairs.shape[1] // 4
    for peer in range(pairs.shape[0]):
        for slot in range(2):
            place = slice(peer * rows, (peer + 1) * rows)
            keys[slot, place] = pairs[peer, slot * rows : (slot + 1) * rows]
            values[slot, place] = pairs[peer, (2 + slot) * rows : (3 + slot) * rows]


def scores_of(keys, queries, bias, scale):
    blocks = bias.shape[0]
    scores = dot(keys, queries, NT) * (scale * LOG2E)
    shaped = scores.reshape(blocks, BLK, queries.shape[0]) + bias[:, None, :]
    return shaped.reshape(scores.shape)


def forward_kernel(members, chunk, scale, bias_ref, pairs, *refs):
    parts, (near, norm_ref, keys, values, queries) = refs[:members], refs[members:]
    load_heads(pairs, keys, values)
    load_queries(parts, queries)
    tokens = queries.shape[1]
    for slot in range(2):
        value_cols = values[slot].T
        for step in range(tokens // chunk):
            rows = slice(step * chunk, (step + 1) * chunk)
            bias = bias_ref[:, span(half_of() * (tokens // chunk) + step, chunk)]
            scores = scores_of(keys[slot], queries[slot, rows], bias, scale)
            top = jnp.max(scores, axis=0, keepdims=True)
            weights = jnp.exp2(scores - top)
            total = jnp.sum(weights, axis=0, keepdims=True)
            probs_low = (weights * (1.0 / total)).astype(jnp.bfloat16)
            place = pl.ds(slot * tokens + step * chunk, chunk)
            near[place] = dot(value_cols, probs_low, NN).T.astype(jnp.bfloat16)
            norm_ref[slot : slot + 1, rows] = top + jnp.log2(total)


def forward(bias, pairs, parts, scale):
    tokens = bias.shape[1]
    chunk = 4 * tokens // pairs.shape[0]
    stats = struct(2, tokens // 2, dtype=jnp.float32)
    return pl.pallas_call(
        functools.partial(forward_kernel, len(parts), chunk, scale),
        out_shape=[struct(tokens, HD), stats],
        in_specs=[VMEM_SPEC] * (2 + len(parts)),
        out_specs=[VMEM_SPEC] * 2,
        scratch_shapes=[VMEM((2, tokens, HD), jnp.bfloat16)] * 2
        + [VMEM((2, tokens // 2, HD), jnp.bfloat16)],
        compiler_params=params(30),
        cost_estimate=cost(),
        name="attend",
    )(bias, pairs, *parts)


def backward_kernel(members, chunk, scale, bias_ref, norm_ref, pairs, near, *refs):
    parts, returns, outs, refs = refs[:members], refs[members], refs[members + 1 : -5], refs[-5:]
    keys, values, queries, grads, query_grad = refs
    load_heads(pairs, keys, values)
    load_queries(parts, queries, grads)
    tokens = queries.shape[1]
    peers = returns.shape[0]
    here = returns.shape[1] // 4
    for slot in range(2):
        key_cols = keys[slot].T
        for step in range(tokens // chunk):
            rows = slice(step * chunk, (step + 1) * chunk)
            bias = bias_ref[:, span(half_of() * (tokens // chunk) + step, chunk)]
            bias = bias - norm_ref[slot : slot + 1, rows]
            probs = jnp.exp2(scores_of(keys[slot], queries[slot, rows], bias, scale))
            prob_grad = dot(values[slot], grads[slot, :, rows], NN)
            delta = jnp.sum(probs * prob_grad, axis=0, keepdims=True)
            score_grad = (probs * (prob_grad - delta)).astype(jnp.bfloat16)
            value_part = dot(probs.astype(jnp.bfloat16), grads[slot, :, rows], NT)
            key_part = dot(score_grad, queries[slot, rows], NN)
            key_total = key_part if step == 0 else key_total + key_part
            value_total = value_part if step == 0 else value_total + value_part
            query_part = dot(key_cols, score_grad, NN) * scale
            query_grad[slot, rows] = query_part.T.astype(jnp.bfloat16)
        for first, total in ((slot, key_total * scale), (2 + slot, value_total)):
            low = total.astype(jnp.bfloat16).reshape(peers, here, HD)
            returns[:, first * here : (first + 1) * here] = low
        for mask, out in enumerate(outs):
            theirs = span(member(mask), here)
            out[slot * here : (slot + 1) * here] = query_grad[slot, theirs]
            theirs = span(slot * len(outs) + member(mask), here)
            out[(2 + slot) * here : (3 + slot) * here] = near[theirs]


def backward(bias, norm, pairs, parts, near, scale):
    peers, tokens = pairs.shape[0], bias.shape[1]
    members = members_of(peers)
    here = tokens // peers
    return pl.pallas_call(
        functools.partial(backward_kernel, members, 4 * here, scale),
        out_shape=[struct(peers, 4 * here, HD)] + [pltpu.HBM((4 * here, HD), jnp.bfloat16)] * members,
        in_specs=[VMEM_SPEC] * (4 + members),
        out_specs=[VMEM_SPEC] * (1 + members),
        scratch_shapes=[VMEM((2, tokens, HD), jnp.bfloat16)] * 2
        + [VMEM((2, tokens // 2, HD), jnp.bfloat16), VMEM((2, HD, tokens // 2), jnp.bfloat16)]
        + [VMEM((2, tokens // 2, HD), jnp.bfloat16)],
        compiler_params=params(30),
        cost_estimate=cost(),
        name="attend_back",
    )(bias, norm, pairs, near, *parts)


def unpack_kernel(returned, *refs):
    queries, (query_grad, key_grad, value_grad, token) = refs[:-4], refs[-4:]
    token[...] = jnp.zeros_like(token)
    members = len(queries)
    here = query_grad.shape[0]
    for index in range(members):
        for slot in range(2):
            columns = pl.ds((index + slot * members) * HD, HD)
            for target, first in ((key_grad, slot), (value_grad, 2 + slot)):
                rows = slice(first * here, (first + 1) * here)
                both = returned[index, rows].astype(jnp.float32) + returned[
                    index + members, rows
                ].astype(jnp.float32)
                target[:, columns] = both.astype(jnp.bfloat16)
            part = queries[index][slot * here : (slot + 1) * here]
            query_grad[:, span(member(index) + slot * members, HD)] = part


def unpack(returned, queries, rows, width):
    return pl.pallas_call(
        unpack_kernel,
        out_shape=[struct(rows, width)] * 3 + [struct(16, HD)],
        in_specs=[VMEM_SPEC] * (1 + len(queries)),
        out_specs=[VMEM_SPEC] * 4,
        compiler_params=params(16),
        cost_estimate=cost(1, 24 * rows * width),
        name="unpack_grads",
    )(returned, *queries)


def join_heads_kernel(*refs):
    parts, attended = refs[:-1], refs[-1]
    rows = attended.shape[0]
    for mask, part in enumerate(parts):
        for slot in range(2):
            columns = span(member(mask) + slot * len(parts), HD)
            attended[:, columns] = part[(2 + slot) * rows : (3 + slot) * rows]


def join_heads(parts):
    rows = parts[0].shape[0] // 4
    return pl.pallas_call(
        join_heads_kernel,
        out_shape=struct(rows, 2 * HD * len(parts)),
        in_specs=[VMEM_SPEC] * len(parts),
        out_specs=VMEM_SPEC,
        compiler_params=params(8),
        cost_estimate=cost(HEADS_FLOPS),
        name="join_heads",
    )(*parts)


def project_kernel(attended, weight_ref, out_ref, token):
    token[...] = jnp.zeros_like(token)
    out_ref[...] = dot(attended[...], weight_ref[...], NN).astype(jnp.bfloat16)


def project(attended, out_weight):
    rows = attended.shape[0]
    depth, width = out_weight.shape
    tile = width // 4
    return pl.pallas_call(
        project_kernel,
        out_shape=[struct(rows, width), struct(16, HD)],
        grid=(width // tile,),
        in_specs=[
            pl.BlockSpec((rows, depth), lambda i: (0, 0)),
            pl.BlockSpec((depth, tile), lambda i: (0, i)),
        ],
        out_specs=[
            pl.BlockSpec((rows, tile), lambda i: (0, i)),
            pl.BlockSpec((16, HD), lambda i: (0, 0)),
        ],
        compiler_params=params(30),
        cost_estimate=cost(PROJECT_FLOPS, 1),
        name="project",
    )(attended, out_weight)


def weight_part_kernel(masks, docs, near, near_pair, *refs):
    grads, out = refs[:-1], refs[-1]
    members = len(grads)
    rows = grads[0].shape[0]
    width = grads[0].shape[1] // docs
    lefts = []
    for source in (near, near_pair):
        for slot in range(2):
            places = [span(slot * members + member(mask), rows) for mask in range(members)]
            lefts.append(jnp.concatenate([source[place] for place in places], axis=0))
    left = jnp.concatenate(lefts, axis=1).T
    for index, mask in enumerate(masks):
        columns = span(lax.axis_index("rep") ^ mask, width)
        right = jnp.concatenate([grad[:, columns] for grad in grads], axis=0)
        place = pl.ds(index * left.shape[0], left.shape[0])
        out[place] = dot(left, right, NN).astype(out.dtype)


def weight_part(near, near_pair, grads, docs, first, dtype):
    masks = range(first, docs, 2)
    width = grads[0].shape[1] // docs
    return pl.pallas_call(
        functools.partial(weight_part_kernel, masks, docs),
        out_shape=struct(len(masks) * 4 * HD, width, dtype=dtype),
        in_specs=[VMEM_SPEC] * (2 + len(grads)),
        out_specs=VMEM_SPEC,
        compiler_params=params(24),
        cost_estimate=cost(),
        name="weight_part",
    )(near, near_pair, *map(in_hbm, grads))


def weight_fold_kernel(own, other, keep, send):
    rows = keep.shape[0]
    keep[...] = own[:rows] + other[:rows].astype(jnp.float32)
    send[...] = (own[rows:] + other[rows:].astype(jnp.float32)).astype(jnp.bfloat16)


def weight_fold(own, other):
    rows, width = own.shape
    return pl.pallas_call(
        weight_fold_kernel,
        out_shape=[struct(rows // 2, width, dtype=jnp.float32), struct(rows // 2, width)],
        in_specs=[VMEM_SPEC] * 2,
        out_specs=[VMEM_SPEC] * 2,
        compiler_params=params(8),
        cost_estimate=cost(),
        name="weight_fold",
    )(own, other)


def weight_spread_kernel(own, other, *targets):
    rows = targets[0].shape[0]
    half = half_of()
    for index, target in enumerate(targets):
        block = span(index // 2 * 2 + (1 - half if index % 2 else half), rows)
        target[...] = (own[block] + other[block].astype(jnp.float32)).astype(target.dtype)


def weight_spread(own, other):
    rows, width = own.shape
    return pl.pallas_call(
        weight_spread_kernel,
        out_shape=[struct(rows // 4, width, dtype=jnp.float32)] + [struct(rows // 4, width)] * 3,
        in_specs=[VMEM_SPEC] * 2,
        out_specs=[VMEM_SPEC] * 4,
        compiler_params=params(8),
        cost_estimate=cost(),
        name="weight_spread",
    )(own, other)


def weight_scale_kernel(factor, first, second, total):
    wide = first[...].astype(jnp.float32) + second[...].astype(jnp.float32)
    total[...] = (wide * factor).astype(jnp.bfloat16)


def weight_scale(anchor, first, second, factor, flops):
    return pl.pallas_call(
        anchored(functools.partial(weight_scale_kernel, factor)),
        out_shape=struct(*first.shape),
        in_specs=[ANY_SPEC] + [VMEM_SPEC] * 2,
        out_specs=VMEM_SPEC,
        compiler_params=params(8),
        cost_estimate=cost(flops),
        name="weight_scale",
    )(anchor, first, second)


def weight_join_kernel(*refs):
    parts, total = refs[:-1], refs[-1]
    width = parts[0].shape[1]
    count = len(parts) // 2
    side = lax.axis_index("seq") & 1
    for index, part in enumerate(parts):
        share = lax.axis_index("rep") ^ (index % count)
        place = side if index < count else 1 - side
        total[:, span(place * count + share, width)] = part[...].astype(jnp.float32)


def weight_join(anchor, parts):
    rows, width = parts[0].shape
    return pl.pallas_call(
        anchored(weight_join_kernel),
        out_shape=struct(rows, width * len(parts), dtype=jnp.float32),
        in_specs=[ANY_SPEC] + [VMEM_SPEC] * len(parts),
        out_specs=VMEM_SPEC,
        compiler_params=params(8),
        cost_estimate=cost(),
        name="weight_join",
    )(anchor, *parts)


def dense_bias(pattern, tokens):
    blocks = pattern.shape[0]
    named = pattern[:, :, None] == jnp.arange(blocks, dtype=pattern.dtype)
    counts = jnp.sum(named.astype(jnp.float32), axis=1).T
    bias = jnp.where(counts > 0, jnp.log2(jnp.maximum(counts, 1.0)), MASKED)
    return jnp.repeat(bias, tokens // blocks, axis=1)


def dense_local(query_in, key_in, value_in, out_weight, grad_out, pattern):
    seq_count, rep_count = lax.axis_size("seq"), lax.axis_size("rep")
    tokens_here = query_in.shape[1]
    tokens = tokens_here * seq_count
    members = members_of(seq_count)
    scale = 1.0 / math.sqrt(HD)
    bias = dense_bias(pattern, tokens)

    pairs = lax.all_to_all(
        pack(key_in[0], value_in[0], seq_count), "seq", split_axis=0, concat_axis=0, tiled=True
    )
    *sends, grad_mine, grad_theirs = head_grads(query_in[0], grad_out[0], out_weight, members)
    parts = [sends[0]] + [swap(sends[mask], "seq", mask) for mask in range(1, members)]
    grad_mine, grad_theirs, *parts[1:2] = after(grad_mine, grad_theirs, *parts[1:2])
    half_grads = {1: swap(grad_theirs, "seq", 1)}
    grad_mine, grad_theirs, *parts[2:3] = after(grad_mine, grad_theirs, *parts[2:3])
    half_grads |= {
        mask: swap(grad_theirs if mask & 1 else grad_mine, "seq", mask) for mask in range(2, members)
    }
    half_grads = [grad_mine] + [half_grads[mask] for mask in range(1, members)]

    near, norm = forward(bias, pairs, parts, scale)
    near_pair = swap(near, "seq", 1)
    returns, *sends = backward(bias, norm, pairs, parts, near, scale)
    near, returns = after(near, returns)
    returned = lax.all_to_all(returns, "seq", split_axis=0, concat_axis=0, tiled=True)
    parts = [sends[0]] + [swap(sends[mask], "seq", mask) for mask in range(1, members)]

    send = weight_part(near, near_pair, half_grads, rep_count, 1, jnp.bfloat16)
    own = weight_part(near, near_pair, half_grads, rep_count, 0, jnp.float32)
    bit = 1
    while 2 * bit < rep_count:
        own, send = weight_fold(own, swap(send, "rep", bit))
        bit *= 2
    own, *sends = weight_spread(own, swap(send, "rep", bit))
    arrived = [swap(block, "seq", mask) for block, mask in zip(sends, (members, 1, members + 1))]
    mixed_out, token = project(join_heads(parts), out_weight)
    factor = 1.0 / math.sqrt(rep_count * tokens)
    mine = weight_scale(token, own, arrived[0], factor, 1)
    other = weight_scale(token, arrived[1], arrived[2], factor, SCALE_FLOPS)
    query_grad, key_grad, value_grad, token = unpack(
        returned, parts, tokens_here, query_in.shape[2]
    )
    shares = []
    for share in (mine, other):
        across, token = after(swap(share, "rep", 2), token)
        shares += [share, swap(share, "rep", 1), across, swap(across, "rep", 1)]
    weight_grad = weight_join(token, shares)
    return (mixed_out[None], query_grad[None], key_grad[None], value_grad[None], weight_grad)


    return (mixed_out[None], query_grad[None], key_grad[None], value_grad[None], weight_grad)


    return (mixed_out[None], query_grad[None], key_grad[None], value_grad[None], weight_grad)


def local(query_in, key_in, value_in, out_weight, grad_out, pattern):
    seq_count, rep_count = lax.axis_size("seq"), lax.axis_size("rep")
    one_head_each = seq_count * HD == query_in.shape[2] and query_in.shape[0] == 1
    paired = seq_count & (seq_count - 1) == 0 and rep_count == 4
    if one_head_each and paired and seq_count > 2:
        return dense_local(query_in, key_in, value_in, out_weight, grad_out, pattern)
    return general_local(query_in, key_in, value_in, out_weight, grad_out, pattern)


def general_local(query_in, key_in, value_in, out_weight, grad_out, pattern):
    seq_count = lax.axis_size("seq")
    rep_count = lax.axis_size("rep")
    tokens_here = query_in.shape[1]
    width = query_in.shape[2]
    head_size = HD
    head_count = width // head_size
    groups = max(seq_count // head_count, 1)
    per_device = max(head_count // seq_count, 1)
    head_groups = head_count // per_device
    local_blocks = tokens_here // BLK
    group_rows = BLK // groups
    all_blocks = seq_count * local_blocks
    columns = per_device * head_size
    span = pattern.shape[1]
    block_run = math.gcd(all_blocks, 32)
    run_count = all_blocks // block_run
    scale = 1.0 / math.sqrt(head_size)

    def to_heads(source):
        shaped = source.reshape(local_blocks, groups, group_rows, head_groups, columns)
        return shaped.transpose(3, 1, 0, 2, 4).reshape(
            seq_count, local_blocks * group_rows, columns
        )

    def to_tokens(source):
        shaped = source.reshape(head_groups, groups, local_blocks, group_rows, columns)
        return shaped.transpose(2, 1, 3, 0, 4).reshape(tokens_here, width)

    query_local = query_in[0]
    key_local = key_in[0]
    value_local = value_in[0]
    grad_local = grad_out[0]

    def spread(source):
        grouped = source.reshape(tokens_here, head_groups, columns).transpose(1, 0, 2)
        copies = jnp.broadcast_to(grouped[:, None], (head_groups, groups, tokens_here, columns))
        return copies.reshape(seq_count, tokens_here, columns)

    query_heads, key_all, value_all = (
        lax.all_to_all(to_heads(query_local), "seq", split_axis=0, concat_axis=0, tiled=True),
        lax.all_to_all(spread(key_local), "seq", split_axis=0, concat_axis=0, tiled=True),
        lax.all_to_all(spread(value_local), "seq", split_axis=0, concat_axis=0, tiled=True),
    )
    attended_grad = lax.dot_general(
        grad_local, out_weight, (((1,), (1,)), ((), ())), preferred_element_type=jnp.float32
    ).astype(jnp.bfloat16)
    grad_heads = lax.all_to_all(
        to_heads(attended_grad), "seq", split_axis=0, concat_axis=0, tiled=True
    )
    key_blocks = key_all.reshape(all_blocks, BLK, per_device, head_size)
    value_blocks = value_all.reshape(all_blocks, BLK, per_device, head_size)
    query_runs = query_heads.reshape(run_count, block_run, group_rows, per_device, head_size)
    grad_runs = grad_heads.reshape(run_count, block_run, group_rows, per_device, head_size)
    pattern_runs = pattern.reshape(run_count, block_run, span)

    def attend_step(carry, items):
        key_acc, value_acc = carry
        query_run, grad_run, pattern_run = items
        key_gathered = key_blocks[pattern_run].reshape(block_run, span * BLK, per_device, head_size)
        value_gathered = value_blocks[pattern_run].reshape(
            block_run, span * BLK, per_device, head_size
        )
        scores = (
            jnp.einsum(
                "crhd,ckhd->chrk", query_run, key_gathered, preferred_element_type=jnp.float32
            )
            * scale
        )
        shifted = scores - jnp.max(scores, axis=-1, keepdims=True)
        weights = jnp.exp(shifted)
        probs = weights / jnp.sum(weights, axis=-1, keepdims=True)
        probs_low = probs.astype(jnp.bfloat16)
        result = jnp.einsum(
            "chrk,ckhd->crhd", probs_low, value_gathered, preferred_element_type=jnp.float32
        ).astype(jnp.bfloat16)
        prob_grad = jnp.einsum(
            "crhd,ckhd->chrk", grad_run, value_gathered, preferred_element_type=jnp.float32
        )
        delta = jnp.sum(probs * prob_grad, axis=-1, keepdims=True)
        score_grad = (probs * (prob_grad - delta)).astype(jnp.bfloat16)
        query_part = (
            jnp.einsum(
                "chrk,ckhd->crhd", score_grad, key_gathered, preferred_element_type=jnp.float32
            )
            * scale
        ).astype(jnp.bfloat16)
        key_contrib = (
            jnp.einsum("chrk,crhd->ckhd", score_grad, query_run, preferred_element_type=jnp.float32)
            * scale
        )
        value_contrib = jnp.einsum(
            "chrk,crhd->ckhd", probs_low, grad_run, preferred_element_type=jnp.float32
        )
        key_acc = key_acc.at[pattern_run].add(
            key_contrib.reshape(block_run, span, BLK, per_device, head_size)
        )
        value_acc = value_acc.at[pattern_run].add(
            value_contrib.reshape(block_run, span, BLK, per_device, head_size)
        )
        return ((key_acc, value_acc), (result, query_part))

    zero_grads = jnp.zeros((all_blocks, BLK, per_device, head_size), jnp.float32)
    (key_acc, value_acc), (out_heads, query_parts) = lax.scan(
        attend_step, (zero_grads, zero_grads), (query_runs, grad_runs, pattern_runs)
    )
    out_send = out_heads.reshape(seq_count, local_blocks * group_rows, columns)
    attended = to_tokens(lax.all_to_all(out_send, "seq", split_axis=0, concat_axis=0, tiled=True))
    mixed_out = jnp.dot(attended, out_weight, preferred_element_type=jnp.float32).astype(
        jnp.bfloat16
    )
    norm_factor = 1.0 / math.sqrt(rep_count * seq_count * tokens_here)
    weight_shard = lax.psum_scatter(
        lax.dot_general(
            attended, grad_local, (((0,), (0,)), ((), ())), preferred_element_type=jnp.float32
        ),
        ("seq", "rep"),
        scatter_dimension=0,
        tiled=True,
    )
    weight_grad = lax.all_gather(
        (weight_shard * norm_factor).astype(jnp.bfloat16), "rep", axis=0, tiled=True
    ).astype(jnp.float32)
    query_send = query_parts.reshape(seq_count, local_blocks * group_rows, columns)
    key_send = key_acc.astype(jnp.bfloat16).reshape(seq_count, tokens_here, columns)
    value_send = value_acc.astype(jnp.bfloat16).reshape(seq_count, tokens_here, columns)
    query_back, key_back, value_back = (
        lax.all_to_all(query_send, "seq", split_axis=0, concat_axis=0, tiled=True),
        lax.all_to_all(key_send, "seq", split_axis=0, concat_axis=0, tiled=True),
        lax.all_to_all(value_send, "seq", split_axis=0, concat_axis=0, tiled=True),
    )

    def fold_groups(source):
        summed = jnp.sum(
            source.reshape(head_groups, groups, tokens_here, columns).astype(jnp.float32), axis=1
        )
        return summed.astype(jnp.bfloat16).transpose(1, 0, 2).reshape(tokens_here, width)

    query_grad = to_tokens(query_back)
    key_grad = fold_groups(key_back)
    value_grad = fold_groups(value_back)
    return (mixed_out[None], query_grad[None], key_grad[None], value_grad[None], weight_grad)


def solution(mesh):
    placed = (
        P("rep", "seq", None),
        P("rep", "seq", None),
        P("rep", "seq", None),
        P(),
        P("rep", "seq", None),
        P(),
    )
    return jax.shard_map(
        local,
        mesh=mesh,
        in_specs=placed,
        out_specs=(
            P("rep", "seq", None),
            P("rep", "seq", None),
            P("rep", "seq", None),
            P("rep", "seq", None),
            P("seq", None),
        ),
        check_vma=False,
    )
```
